32 devices in a mesh: groups: 2 (over x), tiles: 16 (over z, y, core).
Axes of the slice: x: 2, y: 2, z: 4, core: 2. Of those that a mesh axis runs over, the one named last changes fastest.
Arguments:
- input_field: bfloat16 [64, 32, 32, 256], P(('groups', 'tiles')), parts along dimension 0, may hold values from -6 to 6
- cotangent: bfloat16 [64, 32, 32, 256], P(('groups', 'tiles')), parts along dimension 0, may hold values from -6 to 6
- weight: bfloat16 [9, 256, 256], replicated, may hold values from -0.125 to 0.125
- neighbours: int32 [32, 8], P('tiles'), may hold values from -1 to 31, as said below
- land_mask: int32 [32, 32, 32], P('tiles'), may hold values from 0 to 1, as said below
Outputs:
- layer_output: bfloat16 [64, 32, 32, 256], P(('groups', 'tiles')), parts along dimension 0
- input_grad: bfloat16 [64, 32, 32, 256], P(('groups', 'tiles')), parts along dimension 0
- weight_grad: float32 [512, 2304], P(('groups', 'tiles')), parts along dimension 0
The draws below stay inside these ranges and needn't reach their ends.
There are 2 independent parts, one for each index of `groups`. The reference program is written for one: setup_inputs(seed, part) draws one part's arguments, and reference() takes and returns one part's arrays. A program takes and returns all parts, laid end to end along the dimension named above; an argument that names none is the same for every part. Nothing has to cross between parts.
Inputs may be any that keep to these rules, and one draw needn't show every extreme that they name: Device i of the tile axis holds the ocean tiles of tile column i of a band of 4 tile rows, in its first slots, 1 to 2 of them; the last device holds 2; other slots are empty. A row lists the global slot (device index times 2 plus slot) of the tile's neighbours in the order north, south, west, east, north-west, north-east, south-west, south-east, or -1 where there is none (land tile, edge of the band, or an empty slot). West and east wrap around the columns, so every neighbour lies on the same device (north, south) or on the device of index one lower (west side) or one higher (east side), wrapping. `land_mask`: all zero in empty slots.
All inputs are finite; a program needn't handle non-finite values.
Results may differ from the reference program's by a relative error of at most 0.0032.
Values may be sent and summed in bfloat16 or wider, within the bound.
No kernel may reach another device: no remote copies, remote signals or barrier semaphores. Data moves between devices by JAX's collectives and lax.ppermute only.
A program may use at most 128 MiB of HBM per device.

```python
import math
import jax
import jax.numpy as jnp
from jax import lax

PACKED_CHANNELS = 256
TILE_SIDE_CELLS = 32
DILATION_STEP = 2
LAT_TILES = 4
SLOTS = 2
TOTAL_SLOTS = 32
N_TILES = 16


def tile_layout(key):
    count_key, start_key, order_key = jax.random.split(key, 3)
    counts = jax.random.randint(count_key, (N_TILES,), 1, SLOTS + 1)
    columns = jnp.arange(N_TILES)
    counts = jnp.where(columns == N_TILES - 1, SLOTS, counts)
    orders = jax.vmap(lambda column_key: jax.random.permutation(column_key, LAT_TILES))(jax.random.split(order_key, N_TILES))
    tile_rows = orders[:, :SLOTS]
    first_row = jax.random.randint(start_key, (), 0, LAT_TILES - SLOTS + 1)
    tile_rows = tile_rows.at[N_TILES - 1].set(first_row + jnp.arange(SLOTS))
    occupied = jnp.arange(SLOTS)[None, :] < counts[:, None]
    return (tile_rows, occupied)


def draw_neighbours(key, part):
    tile_rows, occupied = tile_layout(key)
    latitudes = jnp.arange(LAT_TILES)
    matches = (tile_rows[:, :, None] == latitudes[None, None, :]) & occupied[:, :, None]
    global_slot = jnp.arange(N_TILES)[:, None] * SLOTS + jnp.arange(SLOTS)[None, :]
    holder = jnp.sum(jnp.where(matches, global_slot[:, :, None] + 1, 0), axis=1) - 1
    directions = [(-1, 0), (1, 0), (0, -1), (0, 1), (-1, -1), (-1, 1), (1, -1), (1, 1)]
    columns_out = []
    for row_step, col_step in directions:
        target_row = tile_rows + row_step
        inside = (target_row >= 0) & (target_row < LAT_TILES)
        target_col = (jnp.arange(N_TILES)[:, None] + col_step) % N_TILES
        holder_slot = holder[target_col, jnp.clip(target_row, 0, LAT_TILES - 1)]
        columns_out.append(jnp.where(inside & occupied, holder_slot, -1))
    table = jnp.stack(columns_out, axis=-1)
    return table.reshape(N_TILES * SLOTS, 8).astype(jnp.int32)


def draw_land_mask(key, part):
    tile_rows, occupied = tile_layout(key)
    key = jax.random.fold_in(key, 12)
    ocean_cells = jax.random.randint(key, (N_TILES * SLOTS, TILE_SIDE_CELLS, TILE_SIDE_CELLS), 0, 10) < 8
    occupied_flat = occupied.reshape(N_TILES * SLOTS)
    return (ocean_cells & occupied_flat[:, None, None]).astype(jnp.int32)


def spiked(drawn, key, source, target, parts, factor):
    owner, partner = [(jnp.arange(drawn.shape[dim]) // (drawn.shape[dim] // parts)).reshape([-1 if axis == dim else 1 for axis in range(drawn.ndim)]) for dim in (source, target)]
    chosen = jax.random.permutation(key, parts)[partner]
    strong = (owner == chosen) | (owner == (partner + parts // 2) % parts)
    return jnp.where(strong, factor * drawn, drawn)


def level_of(key, shape, cuts, low, top_value):
    def one(dim, parts):
        draws = jax.random.uniform(jax.random.fold_in(jax.random.fold_in(key, 6), dim), (parts,), jnp.float32, low / len(cuts), top_value / len(cuts))
        return jnp.repeat(jnp.exp(draws), shape[dim] // parts).reshape((-1,) + (1,) * (len(shape) - dim - 1))

    loudness = one(*cuts[0])
    for cut in cuts[1:]:
        loudness = loudness * one(*cut)
    return loudness


def gaussian(own_key, dims, deviation, limit, pieces=(), kind=jnp.bfloat16):
    entries = deviation * jax.random.normal(own_key, dims, jnp.float32)
    if pieces:
        entries = entries * level_of(own_key, dims, pieces, -0.22, 0.18)
    return jnp.clip(entries, -limit, limit).astype(kind)


def heavy_noise(own_key, dims, spread, most, cuts, heavy, held_as=jnp.bfloat16):
    entries = spread * jax.random.normal(own_key, dims, jnp.float32)
    if cuts:
        entries = entries * level_of(own_key, dims, cuts, -0.22, 0.18)
    return jnp.clip(spiked(entries, jax.random.fold_in(own_key, 3), *heavy), -most, most).astype(held_as)


def setup_inputs(seed: int = 0, part: int = 0) -> dict:
    keys = jax.random.split(jax.random.key(seed), 6)
    part_splits = jax.random.split(jax.random.fold_in(keys[5], part), 6)
    return {
        "input_field": gaussian(part_splits[0], (TOTAL_SLOTS, TILE_SIDE_CELLS, TILE_SIDE_CELLS, PACKED_CHANNELS), 1.0, 6.0, ((0, 16),)),
        "cotangent": heavy_noise(part_splits[1], (TOTAL_SLOTS, TILE_SIDE_CELLS, TILE_SIDE_CELLS, PACKED_CHANNELS), 1.0, 6.0, ((0, 16),), (0, 3, 16, 2.0)),
        "weight": gaussian(keys[2], (9, PACKED_CHANNELS, PACKED_CHANNELS), (9 * PACKED_CHANNELS) ** -0.5, 0.125),
        "neighbours": draw_neighbours(jax.random.fold_in(keys[5], 71), part),
        "land_mask": draw_land_mask(jax.random.fold_in(keys[5], 71), part),
    }


GELU_SCALE = math.sqrt(2.0 / math.pi)
GELU_CUBIC = 0.044715

def gelu_pair(hidden_state):
    tanh_arg = GELU_SCALE * (hidden_state + GELU_CUBIC * hidden_state * hidden_state * hidden_state)
    tanh_value = jnp.tanh(tanh_arg)
    activated = 0.5 * hidden_state * (1.0 + tanh_value)
    derivative = 0.5 * (1.0 + tanh_value) + 0.5 * hidden_state * (1.0 - tanh_value * tanh_value) * GELU_SCALE * (1.0 + 3.0 * GELU_CUBIC * hidden_state * hidden_state)
    return (activated, derivative)

def tap_displacements(dilation):
    return [((row_step - 1) * dilation, (col_step - 1) * dilation) for row_step in range(3) for col_step in range(3)]

def surround_every_tile(source, neighbours, halo_margin_width):
    slot_total = source.shape[0]
    tile_edge = source.shape[1]
    inner_cut = tile_edge - halo_margin_width
    present = neighbours >= 0
    slot_ids = jnp.clip(neighbours, 0, slot_total - 1).astype(jnp.int32)

    def pick_part(part_source, column):
        chosen = jnp.take(part_source, slot_ids[:, column], axis=0)
        return chosen * present[:, column][:, None, None, None].astype(source.dtype)
    north_strip = pick_part(source[:, inner_cut:], 0)
    south_strip = pick_part(source[:, :halo_margin_width], 1)
    west_strip = pick_part(source[:, :, inner_cut:], 2)
    east_strip = pick_part(source[:, :, :halo_margin_width], 3)
    north_west = pick_part(source[:, inner_cut:, inner_cut:], 4)
    north_east = pick_part(source[:, inner_cut:, :halo_margin_width], 5)
    south_west = pick_part(source[:, :halo_margin_width, inner_cut:], 6)
    south_east = pick_part(source[:, :halo_margin_width, :halo_margin_width], 7)
    upper_band = jnp.concatenate([north_west, north_strip, north_east], axis=2)
    middle = jnp.concatenate([west_strip, source, east_strip], axis=2)
    lower_band = jnp.concatenate([south_west, south_strip, south_east], axis=2)
    return jnp.concatenate([upper_band, middle, lower_band], axis=1)

def tile_convolve(haloed_field, weight, start, span, offsets, transposed):
    channels = haloed_field.shape[-1]
    accumulated = jnp.zeros((span * span, weight.shape[1]), jnp.float32)
    for tap_index, (row_displacement, column_shift) in enumerate(offsets):
        shifted_window = haloed_field[start + row_displacement:start + row_displacement + span, start + column_shift:start + column_shift + span].reshape(span * span, channels)
        matrix = weight[tap_index].T if transposed else weight[tap_index]
        accumulated = accumulated + jnp.dot(shifted_window, matrix, preferred_element_type=jnp.float32)
    return accumulated.reshape(span, span, -1)

def reference(input_field, cotangent, weight, neighbours, land_mask):
    ocean_half = land_mask.astype(jnp.bfloat16)[..., None]
    ocean_full = land_mask.astype(jnp.float32)[..., None]
    ocean_masked_input = input_field * ocean_half
    masked_cotangent = cotangent * ocean_half
    forward_tap_list = tap_displacements(DILATION_STEP)
    backward_tap_list = [(-row_displacement, -column_shift) for row_displacement, column_shift in forward_tap_list]
    haloed_input = surround_every_tile(ocean_masked_input, neighbours, DILATION_STEP)

    def forward_tile(operands):
        haloed_field, source, masked_cot, ocean = operands
        hidden_state = tile_convolve(haloed_field, weight, DILATION_STEP, TILE_SIDE_CELLS, forward_tap_list, False)
        activated, derivative = gelu_pair(hidden_state)
        output = (ocean * (source.astype(jnp.float32) + activated)).astype(jnp.bfloat16)
        grad_hidden = (masked_cot.astype(jnp.float32) * derivative).astype(jnp.bfloat16)
        return (output, grad_hidden)
    layer_output, hidden_gradient = lax.map(forward_tile, (haloed_input, input_field, masked_cotangent, ocean_full))
    haloed_gradient = surround_every_tile(hidden_gradient, neighbours, DILATION_STEP)

    def backward_tile(carry, operands):
        gradient_with_halo, input_with_halo, raw_cot, ocean = operands
        backward_pass = tile_convolve(gradient_with_halo, weight, DILATION_STEP, TILE_SIDE_CELLS, backward_tap_list, True)
        grad_tile = (ocean * (raw_cot.astype(jnp.float32) + backward_pass)).astype(jnp.bfloat16)
        gradient_center = gradient_with_halo[DILATION_STEP:DILATION_STEP + TILE_SIDE_CELLS, DILATION_STEP:DILATION_STEP + TILE_SIDE_CELLS].reshape(TILE_SIDE_CELLS * TILE_SIDE_CELLS, PACKED_CHANNELS)
        updates = []
        for row_displacement, column_shift in forward_tap_list:
            shifted_window = input_with_halo[DILATION_STEP + row_displacement:DILATION_STEP + row_displacement + TILE_SIDE_CELLS, DILATION_STEP + column_shift:DILATION_STEP + column_shift + TILE_SIDE_CELLS].reshape(TILE_SIDE_CELLS * TILE_SIDE_CELLS, PACKED_CHANNELS)
            updates.append(jnp.dot(gradient_center.T, shifted_window, preferred_element_type=jnp.float32))
        return (carry + jnp.stack(updates, axis=1), grad_tile)
    initial = jnp.zeros((PACKED_CHANNELS, 9, PACKED_CHANNELS), jnp.float32)
    summed, input_grad = lax.scan(backward_tile, initial, (haloed_gradient, haloed_input, cotangent, ocean_full))
    weight_grad = summed.reshape(PACKED_CHANNELS, 9 * PACKED_CHANNELS) * (1.0 / (TILE_SIDE_CELLS * math.sqrt(TOTAL_SLOTS)))
    return (layer_output, input_grad, weight_grad)
```

```python
import functools
import math

import jax
import jax.numpy as jnp
from jax import lax
from jax.experimental import pallas as pl
from jax.experimental.pallas import tpu as pltpu
from jax.sharding import PartitionSpec as P

STEP = 2
BF16 = jnp.bfloat16
F32 = jnp.float32
GELU_SCALE = math.sqrt(2.0 / math.pi)
GELU_CUBIC = 0.044715
VMEM_BYTES = 16 << 20

SMEM = pl.BlockSpec(memory_space=pltpu.SMEM)
VMEM = pl.BlockSpec(memory_space=pltpu.VMEM)


def gelu_pair(h):
    h2 = h * h
    t = jnp.tanh(h * (GELU_SCALE + (GELU_SCALE * GELU_CUBIC) * h2))
    half_up = 0.5 + 0.5 * t
    activated = h * half_up
    derivative = half_up + h * (0.5 - 0.5 * t * t) * (
        GELU_SCALE + (3.0 * GELU_CUBIC * GELU_SCALE) * h2
    )
    return activated, derivative


def present_bf16(entry):
    return jnp.where(entry >= 0, 1.0, 0.0).astype(BF16)


def column_masks(mask):
    turned = mask.astype(F32).T
    side = turned.shape[0]
    return [
        jnp.broadcast_to(turned[:, r : r + 1], (side, 256)).astype(BF16)
        for r in range(turned.shape[1])
    ]


def edge_selector(rows, cols, picked):
    shape = (len(picked) * rows, rows * cols)
    out = lax.broadcasted_iota(jnp.int32, shape, 0)
    src = lax.broadcasted_iota(jnp.int32, shape, 1)
    want_row = out % rows
    want_col = picked[0] + out // rows
    return jnp.where(src == want_row * cols + want_col, 1.0, 0.0).astype(BF16)


def dot(a, b):
    return jnp.dot(a, b, preferred_element_type=F32)


def interior_kernel(
    local_ref, x_ref, cot_ref, w_ref, mask_ref,
    out_ref, grad_ref, dw_ref, xe_ref, cote_ref,
    xc, mk, gt,
):
    slots, rows, cols, ch = x_ref.shape
    zeros = jnp.zeros((rows, STEP, ch), BF16)
    half = cols // 2
    for s in range(slots):
        for r, line in enumerate(column_masks(mask_ref[s])):
            mk[s, r] = line
        xm = x_ref[s] * mk[s]
        xc[s, STEP : rows + STEP, :, ch : 2 * ch] = xm
        xc[s, STEP : rows + STEP, :, 0:ch] = jnp.concatenate(
            [zeros, xm[:, : cols - STEP]], axis=1
        )
        xc[s, STEP : rows + STEP, :, 2 * ch :] = jnp.concatenate([xm[:, STEP:], zeros], axis=1)
    for s in range(slots):
        north, south = local_ref[s, 0], local_ref[s, 1]
        xc[s, 0:STEP] = xc[jnp.maximum(north, 0), rows : rows + STEP] * present_bf16(north)
        xc[s, rows + STEP :] = xc[jnp.maximum(south, 0), STEP : 2 * STEP] * present_bf16(south)

    block = 8
    column = lax.broadcasted_iota(jnp.int32, (block, cols, ch), 1)
    inside = jnp.where((column >= STEP) & (column < cols - STEP), 1.0, 0.0).astype(BF16)
    for s in range(slots):
        for r0 in range(0, rows, block):
            acc = None
            for a in range(3):
                window = xc[s, r0 + STEP * a : r0 + STEP * a + block].reshape(block * cols, 3 * ch)
                term = dot(window, w_ref[a])
                acc = term if acc is None else acc + term
            activated, derivative = gelu_pair(acc)
            ocean = mk[s, r0 : r0 + block]
            xm = xc[s, r0 + STEP : r0 + STEP + block, :, ch : 2 * ch].reshape(block * cols, ch)
            out = (xm.astype(F32) + activated).astype(BF16).reshape(block, cols, ch)
            out_ref[s, r0 : r0 + block] = out * ocean
            cot = (cot_ref[s, r0 : r0 + block] * ocean) * inside
            g = (cot.reshape(block * cols, ch).astype(F32) * derivative).astype(BF16)
            grad_ref[s, r0 : r0 + block] = g.reshape(block, cols, ch)
            gt[s, :, r0 * cols : (r0 + block) * cols] = g.T

    for a in range(3):
        total = None
        for s in range(slots):
            window = xc[s, STEP * a : STEP * a + rows].reshape(rows * cols, 3 * ch)
            term = dot(gt[s], window)
            total = term if total is None else total + term
        dw_ref[:, a * 3 * ch : (a + 1) * 3 * ch] = total

    for s in range(slots):
        for side, picked in ((0, range(0, 4)), (1, range(half - 4, half))):
            lo = side * half
            xm = xc[s, STEP : rows + STEP, lo : lo + half, ch : 2 * ch].reshape(rows * half, ch)
            sel = edge_selector(rows, half, list(picked))
            xe_ref[s, side * 4 : side * 4 + 4] = (
                dot(sel, xm).astype(BF16).reshape(4, rows, ch)
            )
            cot = (cot_ref[s, :, lo : lo + half] * mk[s, :, lo : lo + half]).reshape(
                rows * half, ch
            )
            outer = sel[: 2 * rows] if side == 0 else sel[2 * rows :]
            cote_ref[side, s] = dot(outer, cot).astype(BF16).reshape(2, rows, ch)


def stack_rows(own, north, south, entry_n, entry_s):
    rows = own.shape[1]
    above = north[:, rows - STEP :] * present_bf16(entry_n)
    below = south[:, :STEP] * present_bf16(entry_s)
    return jnp.concatenate([above, own, below], axis=1)


def edge_kernel(
    local_ref, fw_ref, fe_ref, xe_ref, cote_ref, w_ref, dwi_ref,
    ge_ref, oe_ref, dw_ref,
    win, gt,
):
    slots, _, rows, ch = xe_ref.shape
    for s in range(slots):
        for side in range(2):
            for b in range(3):
                halo = (side == 0 and b == 0) or (side == 1 and b == 2)
                if halo:
                    src = fw_ref if side == 0 else fe_ref
                    mid, top, low = (2, 4, 6) if side == 0 else (3, 5, 7)
                    e_mid, e_top, e_low = local_ref[s, mid], local_ref[s, top], local_ref[s, low]
                    own = src[jnp.maximum(e_mid, 0)] * present_bf16(e_mid)
                    north = src[jnp.maximum(e_top, 0)]
                    south = src[jnp.maximum(e_low, 0)]
                else:
                    first = 2 * (b - 1) if side == 0 else 4 + 2 * b
                    e_top, e_low = local_ref[s, 0], local_ref[s, 1]
                    own = xe_ref[s, first : first + 2]
                    north = xe_ref[jnp.maximum(e_top, 0), first : first + 2]
                    south = xe_ref[jnp.maximum(e_low, 0), first : first + 2]
                tall = stack_rows(own, north, south, e_top, e_low)
                for a in range(3):
                    win[a, side, s, :, :, b * ch : (b + 1) * ch] = tall[
                        :, STEP * a : STEP * a + rows
                    ]
    cells = 2 * slots * 2 * rows
    acc = None
    for a in range(3):
        term = dot(win[a].reshape(cells, 3 * ch), w_ref[a])
        acc = term if acc is None else acc + term
    activated, derivative = gelu_pair(acc)
    x_own = win[1, :, :, :, :, ch : 2 * ch].reshape(cells, ch)
    oe_ref[...] = (x_own.astype(F32) + activated).astype(BF16).reshape(oe_ref.shape)
    g = (cote_ref[...].reshape(cells, ch).astype(F32) * derivative).astype(BF16)
    ge_ref[...] = g.reshape(ge_ref.shape)
    gt[...] = g.T
    for a in range(3):
        span = slice(a * 3 * ch, (a + 1) * 3 * ch)
        dw_ref[:, span] = dwi_ref[:, span] + dot(gt[...], win[a].reshape(cells, 3 * ch))


def spread_selector(rows, cols, first):
    shape = (rows * cols, 2 * rows)
    out = lax.broadcasted_iota(jnp.int32, shape, 0)
    src = lax.broadcasted_iota(jnp.int32, shape, 1)
    want = (out % cols - first) * rows + out // cols
    return jnp.where((src == want) & (out % cols >= first) & (out % cols < first + 2), 1.0, 0.0).astype(BF16)


def input_grad_kernel(
    local_ref, gi_ref, oi_ref, ge_ref, oe_ref, hw_ref, he_ref, cot_ref, w_ref, mask_ref,
    out_ref, ig_ref,
    gc, mk, hs,
):
    slots, rows, cols, ch = gi_ref.shape
    half = cols // 2
    zeros = jnp.zeros((rows, STEP, ch), BF16)
    low = spread_selector(rows, half, 0)
    high = spread_selector(rows, half, half - 2)

    def spread(sel, edge):
        return dot(sel, edge.reshape(2 * rows, ch)).astype(BF16).reshape(rows, half, ch)

    column = lax.broadcasted_iota(jnp.int32, (rows, half, ch), 1)
    for s in range(slots):
        for r, line in enumerate(column_masks(mask_ref[s])):
            mk[s, r] = line
        out_low = jnp.where(column < STEP, spread(low, oe_ref[0, s]), oi_ref[s, :, :half])
        out_ref[s, :, :half] = out_low * mk[s, :, :half]
        out_high = jnp.where(
            column >= half - STEP, spread(high, oe_ref[1, s]), oi_ref[s, :, half:]
        )
        out_ref[s, :, half:] = out_high * mk[s, :, half:]
        g = jnp.concatenate(
            [
                gi_ref[s, :, :half] + spread(low, ge_ref[0, s]),
                gi_ref[s, :, half:] + spread(high, ge_ref[1, s]),
            ],
            axis=1,
        )
        gc[s, STEP : rows + STEP, :, ch : 2 * ch] = g
        gc[s, STEP : rows + STEP, :, 2 * ch :] = jnp.concatenate(
            [zeros, g[:, : cols - STEP]], axis=1
        )
        gc[s, STEP : rows + STEP, :, 0:ch] = jnp.concatenate([g[:, STEP:], zeros], axis=1)
        hs[0, s] = spread(low, hw_ref[s])
        hs[1, s] = spread(high, he_ref[s])
    for s in range(slots):
        north, south = local_ref[s, 0], local_ref[s, 1]
        gc[s, 0:STEP] = gc[jnp.maximum(north, 0), rows : rows + STEP] * present_bf16(north)
        gc[s, rows + STEP :] = gc[jnp.maximum(south, 0), STEP : 2 * STEP] * present_bf16(south)
    for s in range(slots):
        for side, (mid, top, low_entry), lanes, lo in (
            (0, (2, 4, 6), 2 * ch, 0),
            (1, (3, 5, 7), 0, half),
        ):
            def piece(entry, first, count):
                entry = local_ref[s, entry]
                return hs[side, jnp.maximum(entry, 0), first : first + count] * present_bf16(entry)

            halo = jnp.concatenate(
                [piece(top, rows - STEP, STEP), piece(mid, 0, rows), piece(low_entry, 0, STEP)],
                axis=0,
            )
            gc[s, :, lo : lo + half, lanes : lanes + ch] += halo
    block = 8
    for s in range(slots):
        for r0 in range(0, rows, block):
            acc = None
            for a in range(3):
                first = r0 + STEP * (2 - a)
                for b in range(3):
                    window = gc[s, first : first + block, :, b * ch : (b + 1) * ch].reshape(
                        block * cols, ch
                    )
                    term = lax.dot_general(
                        window,
                        w_ref[a, b * ch : (b + 1) * ch],
                        (((1,), (1,)), ((), ())),
                        preferred_element_type=F32,
                    )
                    acc = term if acc is None else acc + term
            cot = cot_ref[s, r0 : r0 + block].reshape(block * cols, ch).astype(F32)
            ig = (cot + acc).astype(BF16).reshape(block, cols, ch)
            ig_ref[s, r0 : r0 + block] = ig * mk[s, r0 : r0 + block]


def permute(value, pairs_of):
    count = lax.axis_size("tiles")
    return lax.ppermute(value, "tiles", [(i, pairs_of(i, count)) for i in range(count)])


def stage_sizes(count):
    rest = count // 2
    middle = 1
    while middle * middle * 4 <= rest:
        middle *= 2
    return rest // middle, middle, 2


def exchange_sum(total, axis, position, size, stride):
    acc = lax.dynamic_index_in_dim(total, position, axis, False)
    parts = []
    for k in range(1, size):
        other = lax.dynamic_index_in_dim(total, position ^ k, axis, False).astype(BF16)
        parts.append(permute(other, lambda i, n: i ^ (k * stride)))
    for part in parts:
        acc = acc + part.astype(F32)
    return acc


def scatter_sum(dw, device):
    count = lax.axis_size("tiles")
    outer, middle, core = stage_sizes(count)
    own_rows = dw.shape[0] // count
    total = dw.reshape(outer, middle, core, own_rows, dw.shape[1])
    c, y, z = device % core, device // core % middle, device // (core * middle)
    total = exchange_sum(total, 2, c, core, 1)
    total = exchange_sum(total, 1, y, middle, core)
    return exchange_sum(total, 0, z, outer, core * middle)


def turned_edge(field, mask, first):
    edge = field[:, :, first : first + STEP] * mask[:, :, first : first + STEP, None].astype(BF16)
    return edge.transpose(0, 2, 1, 3)


def shards(input_field, cotangent, weight, neighbours, land_mask):
    device = lax.axis_index("tiles")
    count = lax.axis_size("tiles")
    slots, rows, cols, ch = input_field.shape
    taps = weight.reshape(3, 3 * ch, ch)
    bases = jnp.stack(
        [device, device, (device - 1) % count, (device + 1) % count] + [(device - 1) % count, (device + 1) % count] * 2
    ) * slots
    local = jnp.where(neighbours >= 0, jnp.clip(neighbours - bases[None, :], 0, slots - 1), -1)
    params = pltpu.CompilerParams(vmem_limit_bytes=VMEM_BYTES)

    east_edge = turned_edge(input_field, land_mask, cols - STEP)
    west_edge = turned_edge(input_field, land_mask, 0)
    from_west = permute(east_edge, lambda i, n: (i + 1) % n)
    from_east = permute(west_edge, lambda i, n: (i - 1) % n)

    edge = (2, slots, STEP, rows, ch)
    out_inner, grad_inner, dw_inner, x_edge, cot_edge = pl.pallas_call(
        interior_kernel,
        out_shape=(
            jax.ShapeDtypeStruct(input_field.shape, BF16),
            jax.ShapeDtypeStruct(input_field.shape, BF16),
            jax.ShapeDtypeStruct((ch, 9 * ch), F32),
            jax.ShapeDtypeStruct((slots, 8, rows, ch), BF16),
            jax.ShapeDtypeStruct(edge, BF16),
        ),
        in_specs=[SMEM, VMEM, VMEM, VMEM, VMEM],
        out_specs=(VMEM,) * 5,
        scratch_shapes=[
            pltpu.VMEM((slots, rows + 2 * STEP, cols, 3 * ch), BF16),
            pltpu.VMEM((slots, rows, cols, ch), BF16),
            pltpu.VMEM((slots, ch, rows * cols), BF16),
        ],
        compiler_params=params,
        cost_estimate=pl.CostEstimate(
            flops=4 * 9 * slots * rows * cols * ch * ch, bytes_accessed=8 << 20, transcendentals=0
        ),
        name="interior",
    )(local, input_field, cotangent, taps, land_mask)

    grad_edge, out_edge, dw = pl.pallas_call(
        edge_kernel,
        out_shape=(
            jax.ShapeDtypeStruct(edge, BF16),
            jax.ShapeDtypeStruct(edge, BF16),
            jax.ShapeDtypeStruct((ch, 9 * ch), F32),
        ),
        in_specs=[SMEM] + [VMEM] * 6,
        out_specs=(VMEM,) * 3,
        scratch_shapes=[
            pltpu.VMEM((3, 2, slots, STEP, rows, 3 * ch), BF16),
            pltpu.VMEM((ch, 4 * slots * rows), BF16),
        ],
        compiler_params=params,
        cost_estimate=pl.CostEstimate(
            flops=4 * 9 * slots * rows * 4 * ch * ch, bytes_accessed=6 << 20, transcendentals=0
        ),
        name="edges",
    )(local, from_west, from_east, x_edge, cot_edge, taps, dw_inner)

    grad_west = permute(grad_edge[1], lambda i, n: (i + 1) % n)
    grad_east = permute(grad_edge[0], lambda i, n: (i - 1) % n)
    summed = scatter_sum(dw, device)

    layer_output, input_grad = pl.pallas_call(
        input_grad_kernel,
        out_shape=(
            jax.ShapeDtypeStruct(input_field.shape, BF16),
            jax.ShapeDtypeStruct(input_field.shape, BF16),
        ),
        in_specs=[SMEM] + [VMEM] * 9,
        out_specs=(VMEM,) * 2,
        scratch_shapes=[
            pltpu.VMEM((slots, rows + 2 * STEP, cols, 3 * ch), BF16),
            pltpu.VMEM((slots, rows, cols, ch), BF16),
            pltpu.VMEM((2, slots, rows, cols // 2, ch), BF16),
        ],
        compiler_params=params,
        cost_estimate=pl.CostEstimate(
            flops=2 * 9 * slots * rows * cols * ch * ch, bytes_accessed=8 << 20, transcendentals=0
        ),
        name="input_grad",
    )(local, grad_inner, out_inner, grad_edge, out_edge, grad_west, grad_east, cotangent, taps, land_mask)

    scale_factor = 1.0 / (rows * math.sqrt(slots * count))
    return layer_output, input_grad, summed * scale_factor


def solution(mesh):
    return jax.shard_map(
        shards,
        mesh=mesh,
        in_specs=(
            P(("groups", "tiles"), None, None, None),
            P(("groups", "tiles"), None, None, None),
            P(),
            P("tiles", None),
            P("tiles", None, None),
        ),
        out_specs=(
            P(("groups", "tiles"), None, None, None),
            P(("groups", "tiles"), None, None, None),
            P(("groups", "tiles"), None),
        ),
        check_vma=False,
    )
```

```python
import functools
import math

import jax
import jax.numpy as jnp
from jax import lax
from jax.experimental import pallas as pl
from jax.experimental.pallas import tpu as pltpu
from jax.sharding import PartitionSpec as P

STEP = 2
BF16 = jnp.bfloat16
F32 = jnp.float32
GELU_SCALE = math.sqrt(2.0 / math.pi)
GELU_CUBIC = 0.044715
VMEM_BYTES = 16 << 20
LOAD_BYTES = 101 << 19

SMEM = pl.BlockSpec(memory_space=pltpu.SMEM)
VMEM = pl.BlockSpec(memory_space=pltpu.VMEM)
HBM = pl.BlockSpec(memory_space=pltpu.HBM)


def gelu_pair(h):
    h2 = h * h
    t = jnp.tanh(h * (GELU_SCALE + (GELU_SCALE * GELU_CUBIC) * h2))
    half_up = 0.5 + 0.5 * t
    activated = h * half_up
    derivative = half_up + h * (0.5 - 0.5 * t * t) * (
        GELU_SCALE + (3.0 * GELU_CUBIC * GELU_SCALE) * h2
    )
    return activated, derivative


def present_bf16(entry):
    return jnp.where(entry >= 0, 1.0, 0.0).astype(BF16)


def column_masks(mask):
    turned = mask.astype(F32).T
    side = turned.shape[0]
    return [
        jnp.broadcast_to(turned[:, r : r + 1], (side, 256)).astype(BF16)
        for r in range(turned.shape[1])
    ]


def edge_selector(rows, cols, picked):
    shape = (len(picked) * rows, rows * cols)
    out = lax.broadcasted_iota(jnp.int32, shape, 0)
    src = lax.broadcasted_iota(jnp.int32, shape, 1)
    want_row = out % rows
    want_col = picked[0] + out // rows
    return jnp.where(src == want_row * cols + want_col, 1.0, 0.0).astype(BF16)


def dot(a, b):
    return jnp.dot(a, b, preferred_element_type=F32)


def local_id(entry, slots):
    return jnp.where(entry < 0, -1, lax.rem(entry, slots))


def start_all(copies):
    for copy in copies:
        copy.start()
    return copies


def is_even():
    return lax.rem(lax.axis_index("tiles"), 2) == 0


def split_sides(west, east, across_ref, pair_ref):
    even = is_even()
    across_ref[...] = jnp.where(even, west, east).reshape(across_ref.shape)
    pair_ref[...] = jnp.where(even, east, west).reshape(pair_ref.shape)


def join_sides(across, pair):
    even = is_even()
    return jnp.where(even, across, pair), jnp.where(even, pair, across)


def load_kernel(
    x_hbm, cot_hbm, mask_hbm,
    across_ref, pair_ref, xe_ref, cote_ref, x_ref, cot_ref,
    ms, sems,
):
    slots, rows, cols, ch = x_ref.shape
    half = cols // 2
    loads = start_all(
        [pltpu.make_async_copy(mask_hbm, ms, sems.at[0])]
        + [
            pltpu.make_async_copy(src.at[s], dst.at[s], sems.at[1 + i * slots + s])
            for i, (src, dst) in enumerate(((x_hbm, x_ref), (cot_hbm, cot_ref)))
            for s in range(slots)
        ]
    )
    sel = [
        edge_selector(rows, half, list(range(0, 4))),
        edge_selector(rows, half, list(range(half - 4, half))),
    ]
    for copy in loads:
        copy.wait()
    for s in range(slots):
        mask = ms[s].astype(F32)
        for side in range(2):
            lo = 0 if side == 0 else cols - 4
            tiles = slice(side * half, side * half + half)
            ocean = jnp.stack(
                [
                    jnp.broadcast_to(mask[:, lo + k : lo + k + 1], (rows, ch)).astype(BF16)
                    for k in range(4)
                ]
            )
            x = dot(sel[side], x_ref[s, :, tiles].reshape(rows * half, ch)).astype(BF16)
            xe_ref[s, side * 4 : side * 4 + 4] = x.reshape(4, rows, ch) * ocean
            outer = slice(0, 2) if side == 0 else slice(2, 4)
            pick = sel[side][: 2 * rows] if side == 0 else sel[side][2 * rows :]
            c = dot(pick, cot_ref[s, :, tiles].reshape(rows * half, ch)).astype(BF16)
            cote_ref[side, s] = c.reshape(2, rows, ch) * ocean[outer]
    split_sides(xe_ref[:, 0:2], xe_ref[:, 6:8], across_ref, pair_ref)


def interior_kernel(
    own, nbr_ref, x_ref, cot_ref, w_ref, ms,
    out_ref, grad_ref, dw_ref,
    xc, mk, gt,
):
    slots, rows, cols, ch = x_ref.shape
    zeros = jnp.zeros((rows, STEP, ch), BF16)
    for s in range(slots):
        for r, line in enumerate(column_masks(ms[s])):
            mk[s, r] = line
    for s in range(slots):
        xm = x_ref[s] * mk[s]
        xc[s, STEP : rows + STEP, :, ch : 2 * ch] = xm
        xc[s, STEP : rows + STEP, :, 0:ch] = jnp.concatenate(
            [zeros, xm[:, : cols - STEP]], axis=1
        )
        xc[s, STEP : rows + STEP, :, 2 * ch :] = jnp.concatenate([xm[:, STEP:], zeros], axis=1)
    for s in range(slots):
        north, south = local_id(nbr_ref[s, 0], slots), local_id(nbr_ref[s, 1], slots)
        xc[s, 0:STEP] = xc[jnp.maximum(north, 0), rows : rows + STEP] * present_bf16(north)
        xc[s, rows + STEP :] = xc[jnp.maximum(south, 0), STEP : 2 * STEP] * present_bf16(south)

    block = 8
    column = lax.broadcasted_iota(jnp.int32, (block, cols, ch), 1)
    inside = jnp.where((column >= STEP) & (column < cols - STEP), 1.0, 0.0).astype(BF16)
    for s in range(slots):
        for r0 in range(0, rows, block):
            acc = None
            for a in range(3):
                window = xc[s, r0 + STEP * a : r0 + STEP * a + block].reshape(block * cols, 3 * ch)
                term = dot(window, w_ref[a])
                acc = term if acc is None else acc + term
            activated, derivative = gelu_pair(acc)
            ocean = mk[s, r0 : r0 + block]
            xm = xc[s, r0 + STEP : r0 + STEP + block, :, ch : 2 * ch].reshape(block * cols, ch)
            out = (xm.astype(F32) + activated).astype(BF16).reshape(block, cols, ch)
            out_ref[s, r0 : r0 + block] = out * ocean
            cot = (cot_ref[s, r0 : r0 + block] * ocean) * inside
            g = (cot.reshape(block * cols, ch).astype(F32) * derivative).astype(BF16)
            grad_ref[s, r0 : r0 + block] = g.reshape(block, cols, ch)
            turn_rows(gt.at[s], g, r0 * cols, own)

    for a in range(3):
        total = None
        for s in range(slots):
            window = xc[s, STEP * a : STEP * a + rows].reshape(rows * cols, 3 * ch)
            term = dot(gt[s], window)
            total = term if total is None else total + term
        dw_ref[:, :, a * 3 * ch : (a + 1) * 3 * ch] = total.reshape(dw_ref.shape[0], -1, 3 * ch)


def turn_rows(gt, g, first, own):
    turned = g.T
    ch, cells = turned.shape
    if own is None:
        gt[:, first : first + cells] = turned
        return
    for j in range(ch // own):
        to = (j % 2) * (ch // 2) + (j // 2) * own
        gt[to : to + own, first : first + cells] = turned[j * own : (j + 1) * own]


def stack_rows(own, north, south, entry_n, entry_s):
    rows = own.shape[1]
    above = north[:, rows - STEP :] * present_bf16(entry_n)
    below = south[:, :STEP] * present_bf16(entry_s)
    return jnp.concatenate([above, own, below], axis=1)


def edge_kernel(
    own, nbr_ref, across_ref, pair_ref, xe_ref, cote_ref, w_ref, dwi_ref,
    gacross_ref, gpair_ref, ge_ref, oe_ref, *outs,
):
    *dw_refs, sides, win, gt = outs
    slots, _, rows, ch = xe_ref.shape
    device = lax.axis_index("tiles")
    sides[0], sides[1] = join_sides(across_ref[...], pair_ref[...])

    def local(s, column):
        return local_id(nbr_ref[s, column], slots)

    for s in range(slots):
        for side in range(2):
            for b in range(3):
                halo = (side == 0 and b == 0) or (side == 1 and b == 2)
                if halo:
                    src = sides.at[side]
                    mid, top, low = (2, 4, 6) if side == 0 else (3, 5, 7)
                    e_mid, e_top, e_low = local(s, mid), local(s, top), local(s, low)
                    middle = src[jnp.maximum(e_mid, 0)] * present_bf16(e_mid)
                    north = src[jnp.maximum(e_top, 0)]
                    south = src[jnp.maximum(e_low, 0)]
                else:
                    at = 2 * (b - 1) if side == 0 else 4 + 2 * b
                    e_top, e_low = local(s, 0), local(s, 1)
                    middle = xe_ref[s, at : at + 2]
                    north = xe_ref[jnp.maximum(e_top, 0), at : at + 2]
                    south = xe_ref[jnp.maximum(e_low, 0), at : at + 2]
                tall = stack_rows(middle, north, south, e_top, e_low)
                for a in range(3):
                    win[a, side, s, :, :, b * ch : (b + 1) * ch] = tall[
                        :, STEP * a : STEP * a + rows
                    ]
    cells = 2 * slots * 2 * rows
    acc = None
    for a in range(3):
        term = dot(win[a].reshape(cells, 3 * ch), w_ref[a])
        acc = term if acc is None else acc + term
    activated, derivative = gelu_pair(acc)
    x_own = win[1, :, :, :, :, ch : 2 * ch].reshape(cells, ch)
    oe_ref[...] = (x_own.astype(F32) + activated).astype(BF16).reshape(oe_ref.shape)
    g = (cote_ref[...].reshape(cells, ch).astype(F32) * derivative).astype(BF16)
    ge_ref[...] = g.reshape(ge_ref.shape)
    split_sides(g[: cells // 2], g[cells // 2 :], gacross_ref, gpair_ref)
    turn_rows(gt, g, 0, own)
    if own is None:
        (dw_ref,) = dw_refs
        for a in range(3):
            span = slice(a * 3 * ch, (a + 1) * 3 * ch)
            dw_ref[:, span] = dwi_ref[0, :, span] + dot(gt[...], win[a].reshape(cells, 3 * ch))
        return
    keep_ref, send_ref = dw_refs
    core = lax.rem(device, 2)
    rank = ch // 2
    keep_rows = gt[pl.ds(pl.multiple_of(core * rank, rank), rank), :]
    send_rows = gt[pl.ds(pl.multiple_of((1 - core) * rank, rank), rank), :]
    turned = jnp.concatenate([keep_rows, send_rows], axis=0)
    for a in range(3):
        span = slice(a * 3 * ch, (a + 1) * 3 * ch)
        term = dot(turned, win[a].reshape(cells, 3 * ch))
        keep_ref[:, span] = dwi_ref[core, :, span] + term[:rank]
        send_ref[:, span] = (dwi_ref[1 - core, :, span] + term[rank:]).astype(BF16)


def spread_selector(rows, cols, first):
    shape = (rows * cols, 2 * rows)
    out = lax.broadcasted_iota(jnp.int32, shape, 0)
    src = lax.broadcasted_iota(jnp.int32, shape, 1)
    want = (out % cols - first) * rows + out // cols
    return jnp.where((src == want) & (out % cols >= first) & (out % cols < first + 2), 1.0, 0.0).astype(BF16)


def input_grad_kernel(
    nbr_ref, gi_ref, oi_ref, ge_ref, oe_ref, across_ref, pair_ref, cot_ref, w_ref, mask_ref,
    out_hbm, ig_hbm,
    out_ref, ig_ref, gc, mk, hs, sems,
):
    slots, rows, cols, ch = gi_ref.shape
    half = cols // 2
    zeros = jnp.zeros((rows, STEP, ch), BF16)
    low = spread_selector(rows, half, 0)
    high = spread_selector(rows, half, half - 2)
    halos = join_sides(across_ref[...], pair_ref[...])

    def spread(sel, edge):
        return dot(sel, edge.reshape(2 * rows, ch)).astype(BF16).reshape(rows, half, ch)

    column = lax.broadcasted_iota(jnp.int32, (rows, half, ch), 1)
    for s in range(slots):
        for r, line in enumerate(column_masks(mask_ref[s])):
            mk[s, r] = line
        out_low = jnp.where(column < STEP, spread(low, oe_ref[0, s]), oi_ref[s, :, :half])
        out_ref[s, :, :half] = out_low * mk[s, :, :half]
        out_high = jnp.where(
            column >= half - STEP, spread(high, oe_ref[1, s]), oi_ref[s, :, half:]
        )
        out_ref[s, :, half:] = out_high * mk[s, :, half:]
        g = jnp.concatenate(
            [
                gi_ref[s, :, :half] + spread(low, ge_ref[0, s]),
                gi_ref[s, :, half:] + spread(high, ge_ref[1, s]),
            ],
            axis=1,
        )
        gc[s, STEP : rows + STEP, :, ch : 2 * ch] = g
        gc[s, STEP : rows + STEP, :, 2 * ch :] = jnp.concatenate(
            [zeros, g[:, : cols - STEP]], axis=1
        )
        gc[s, STEP : rows + STEP, :, 0:ch] = jnp.concatenate([g[:, STEP:], zeros], axis=1)
        hs[0, s] = spread(low, halos[0][s])
        hs[1, s] = spread(high, halos[1][s])
    stores = start_all(
        [pltpu.make_async_copy(out_ref.at[s], out_hbm.at[s], sems.at[s]) for s in range(slots)]
    )
    for s in range(slots):
        north, south = local_id(nbr_ref[s, 0], slots), local_id(nbr_ref[s, 1], slots)
        gc[s, 0:STEP] = gc[jnp.maximum(north, 0), rows : rows + STEP] * present_bf16(north)
        gc[s, rows + STEP :] = gc[jnp.maximum(south, 0), STEP : 2 * STEP] * present_bf16(south)
    for s in range(slots):
        for side, (mid, top, low_entry), lanes, lo in (
            (0, (2, 4, 6), 2 * ch, 0),
            (1, (3, 5, 7), 0, half),
        ):
            def piece(entry, first, count):
                entry = local_id(nbr_ref[s, entry], slots)
                return hs[side, jnp.maximum(entry, 0), first : first + count] * present_bf16(entry)

            halo = jnp.concatenate(
                [piece(top, rows - STEP, STEP), piece(mid, 0, rows), piece(low_entry, 0, STEP)],
                axis=0,
            )
            gc[s, :, lo : lo + half, lanes : lanes + ch] += halo
    block = 8
    for s in range(slots):
        for r0 in range(0, rows, block):
            acc = None
            for a in range(3):
                first = r0 + STEP * (2 - a)
                for b in range(3):
                    window = gc[s, first : first + block, :, b * ch : (b + 1) * ch].reshape(
                        block * cols, ch
                    )
                    term = lax.dot_general(
                        window,
                        w_ref[a, b * ch : (b + 1) * ch],
                        (((1,), (1,)), ((), ())),
                        preferred_element_type=F32,
                    )
                    acc = term if acc is None else acc + term
            cot = cot_ref[s, r0 : r0 + block].reshape(block * cols, ch).astype(F32)
            ig = (cot + acc).astype(BF16).reshape(block, cols, ch)
            ig_ref[s, r0 : r0 + block] = ig * mk[s, r0 : r0 + block]
        stores += start_all(
            [pltpu.make_async_copy(ig_ref.at[s], ig_hbm.at[s], sems.at[slots + s])]
        )
    for copy in stores:
        copy.wait()


def permute(value, pairs_of):
    count = lax.axis_size("tiles")
    return lax.ppermute(value, "tiles", [(i, pairs_of(i, count)) for i in range(count)])


def swap_halos(across, pair):
    across = permute(across, lambda i, n: (i - 1 if i % 2 == 0 else i + 1) % n)
    return across, permute(pair, lambda i, n: i ^ 1)


def stage_sizes(count):
    rest = count // 2
    middle = 1
    while middle * middle * 4 <= rest:
        middle *= 2
    return rest // middle, middle, 2


def exchange_sum(total, axis, position, size, stride):
    acc = lax.dynamic_index_in_dim(total, position, axis, False)
    parts = []
    for k in range(1, size):
        other = lax.dynamic_index_in_dim(total, position ^ k, axis, False).astype(BF16)
        parts.append(permute(other, lambda i, n: i ^ (k * stride)))
    for part in parts:
        acc = acc + part.astype(F32)
    return acc


def scatter_sum(dw, device):
    count = lax.axis_size("tiles")
    outer, middle, core = stage_sizes(count)
    own_rows = dw.shape[0] // count
    total = dw.reshape(outer, middle, core, own_rows, dw.shape[1])
    c, y, z = device % core, device // core % middle, device // (core * middle)
    total = exchange_sum(total, 2, c, core, 1)
    total = exchange_sum(total, 1, y, middle, core)
    return exchange_sum(total, 0, z, outer, core * middle)


def split_kernel(stride, keep_ref, *refs):
    size = keep_ref.shape[1]
    count = len(refs) - size
    recvs, keep_out, sends = refs[:count], refs[count], refs[count + 1 :]
    place = lax.rem(lax.axis_index("tiles") // stride, size)
    for i in range(keep_ref.shape[0]):
        for k in range(size):
            acc = keep_ref[i, place ^ k]
            for recv in recvs:
                acc = acc + recv[i, place ^ k].astype(F32)
            if k == 0:
                keep_out[i] = acc
            else:
                sends[k - 1][i] = acc.astype(BF16)


def last_kernel(scale, keep_ref, *refs):
    *recvs, out_ref = refs
    acc = keep_ref[...]
    for recv in recvs:
        acc = acc + recv[...].astype(F32)
    out_ref[...] = acc * scale


def small_call(kernel, out_shapes, name, *args):
    return pl.pallas_call(
        kernel,
        out_shape=out_shapes,
        in_specs=[VMEM] * len(args),
        out_specs=tuple(VMEM for _ in out_shapes),
        compiler_params=pltpu.CompilerParams(vmem_limit_bytes=8 << 20),
        name=name,
    )(*args)


def shape_f32(*dims):
    return jax.ShapeDtypeStruct(dims, F32)


def shape_bf16(*dims):
    return jax.ShapeDtypeStruct(dims, BF16)


def shards(input_field, cotangent, weight, neighbours, land_mask):
    device = lax.axis_index("tiles")
    count = lax.axis_size("tiles")
    slots, rows, cols, ch = input_field.shape
    taps = weight.reshape(3, 3 * ch, ch)
    params = pltpu.CompilerParams(vmem_limit_bytes=VMEM_BYTES)
    side_columns = (slots, STEP, rows, ch)
    field = input_field.shape
    own = ch // count if ch // count % 16 == 0 else None
    outer, middle, _ = stage_sizes(count)

    across, pair, x_edge, cot_edge, field_in, cot_in = pl.pallas_call(
        load_kernel,
        out_shape=(
            shape_bf16(*side_columns),
            shape_bf16(*side_columns),
            shape_bf16(slots, 8, rows, ch),
            shape_bf16(2, *side_columns),
            shape_bf16(*field),
            shape_bf16(*field),
        ),
        in_specs=[HBM] * 3,
        out_specs=(VMEM,) * 6,
        scratch_shapes=[
            pltpu.VMEM((slots, rows, cols), jnp.int32),
            pltpu.SemaphoreType.DMA((1 + 2 * slots,)),
        ],
        compiler_params=pltpu.CompilerParams(vmem_limit_bytes=LOAD_BYTES),
        name="load",
    )(input_field, cotangent, land_mask)
    across, pair = swap_halos(across, pair)

    cores = 1 if own is None else 2
    out_inner, grad_inner, dw_inner = pl.pallas_call(
        functools.partial(interior_kernel, own),
        out_shape=(
            shape_bf16(*field),
            shape_bf16(*field),
            shape_f32(cores, ch // cores, 9 * ch),
        ),
        in_specs=[SMEM] + [VMEM] * 4,
        out_specs=(VMEM,) * 3,
        scratch_shapes=[
            pltpu.VMEM((slots, rows + 2 * STEP, cols, 3 * ch), BF16),
            pltpu.VMEM(field, BF16),
            pltpu.VMEM((slots, ch, rows * cols), BF16),
        ],
        compiler_params=params,
        cost_estimate=pl.CostEstimate(
            flops=4 * 9 * slots * rows * cols * ch * ch, bytes_accessed=8 << 20, transcendentals=0
        ),
        name="interior",
    )(neighbours, field_in, cot_in, taps, land_mask)

    if own is None:
        dw_shapes = (shape_f32(ch, 9 * ch),)
    else:
        dw_shapes = (shape_f32(ch // 2, 9 * ch), shape_bf16(ch // 2, 9 * ch))
    grad_across, grad_pair, grad_edge, out_edge, *dw = pl.pallas_call(
        functools.partial(edge_kernel, own),
        out_shape=(
            shape_bf16(*side_columns),
            shape_bf16(*side_columns),
            shape_bf16(2, *side_columns),
            shape_bf16(2, *side_columns),
            *dw_shapes,
        ),
        in_specs=[SMEM] + [VMEM] * 6,
        out_specs=(VMEM,) * (4 + len(dw_shapes)),
        scratch_shapes=[
            pltpu.VMEM((2, *side_columns), BF16),
            pltpu.VMEM((3, 2, slots, STEP, rows, 3 * ch), BF16),
            pltpu.VMEM((ch, 4 * slots * rows), BF16),
        ],
        compiler_params=params,
        cost_estimate=pl.CostEstimate(
            flops=4 * 9 * slots * rows * 4 * ch * ch, bytes_accessed=6 << 20, transcendentals=0
        ),
        name="edges",
    )(neighbours, across, pair, x_edge, cot_edge, taps, dw_inner)

    grad_across, grad_pair = swap_halos(grad_across, grad_pair)

    def input_grad_call():
        return pl.pallas_call(
            input_grad_kernel,
            out_shape=(shape_bf16(*field), shape_bf16(*field)),
            in_specs=[SMEM] + [VMEM] * 9,
            out_specs=(HBM, HBM),
            scratch_shapes=[pltpu.VMEM(field, BF16)] * 2
            + [
                pltpu.VMEM((slots, rows + 2 * STEP, cols, 3 * ch), BF16),
                pltpu.VMEM(field, BF16),
                pltpu.VMEM((2, slots, rows, cols // 2, ch), BF16),
                pltpu.SemaphoreType.DMA((2 * slots,)),
            ],
            compiler_params=params,
            cost_estimate=pl.CostEstimate(
                flops=2 * 9 * slots * rows * cols * ch * ch,
                bytes_accessed=8 << 20,
                transcendentals=0,
            ),
            name="input_grad",
        )(
            neighbours, grad_inner, out_inner, grad_edge, out_edge,
            grad_across, grad_pair, cot_in, taps, land_mask,
        )

    scale_factor = 1.0 / (rows * math.sqrt(slots * count))
    if own is None:
        summed = scatter_sum(dw[0], device)
        return *input_grad_call(), summed * scale_factor

    keep, send = dw
    wide = 9 * ch
    recv = permute(send, lambda i, n: i ^ 1)
    whole = (outer, middle, own, wide)
    keep, *sends = small_call(
        functools.partial(split_kernel, 2),
        (shape_f32(outer, own, wide), *[shape_bf16(outer, own, wide)] * (middle - 1)),
        "middle_terms", keep.reshape(whole), recv.reshape(whole),
    )
    recvs = [permute(sends[k - 1], lambda i, n, k=k: i ^ (k * 2)) for k in range(1, middle)]
    layer_output, input_grad = input_grad_call()
    keep, *recvs, layer_output, input_grad = lax.optimization_barrier(
        (keep, *recvs, layer_output, input_grad)
    )
    keep, *sends = small_call(
        functools.partial(split_kernel, 2 * middle),
        (shape_f32(1, own, wide), *[shape_bf16(1, own, wide)] * (outer - 1)),
        "outer_terms", keep[None], *[recv[None] for recv in recvs],
    )
    recvs = [
        permute(sends[k - 1], lambda i, n, k=k: i ^ (k * 2 * middle))
        for k in reversed(range(1, outer))
    ]
    (summed,) = small_call(
        functools.partial(last_kernel, scale_factor),
        (shape_f32(1, own, wide),),
        "last_sum", keep, *recvs,
    )
    return layer_output, input_grad, summed[0]


def solution(mesh):
    return jax.shard_map(
        shards,
        mesh=mesh,
        in_specs=(
            P(("groups", "tiles"), None, None, None),
            P(("groups", "tiles"), None, None, None),
            P(),
            P("tiles", None),
            P("tiles", None, None),
        ),
        out_specs=(
            P(("groups", "tiles"), None, None, None),
            P(("groups", "tiles"), None, None, None),
            P(("groups", "tiles"), None),
        ),
        check_vma=False,
    )
```

```python
import functools
import math

import jax
import jax.numpy as jnp
from jax import lax
from jax.experimental import pallas as pl
from jax.experimental.pallas import tpu as pltpu
from jax.sharding import PartitionSpec as P

STEP = 2
BF16 = jnp.bfloat16
F32 = jnp.float32
GELU_SCALE = math.sqrt(2.0 / math.pi)
GELU_CUBIC = 0.044715
VMEM_BYTES = 16 << 20
LOAD_BYTES = 101 << 19

SMEM = pl.BlockSpec(memory_space=pltpu.SMEM)
VMEM = pl.BlockSpec(memory_space=pltpu.VMEM)
HBM = pl.BlockSpec(memory_space=pltpu.HBM)


def gelu_pair(h):
    h2 = h * h
    t = jnp.tanh(h * (GELU_SCALE + (GELU_SCALE * GELU_CUBIC) * h2))
    half_up = 0.5 + 0.5 * t
    activated = h * half_up
    derivative = half_up + h * (0.5 - 0.5 * t * t) * (
        GELU_SCALE + (3.0 * GELU_CUBIC * GELU_SCALE) * h2
    )
    return activated, derivative


def present_bf16(entry):
    return jnp.where(entry >= 0, 1.0, 0.0).astype(BF16)


def column_masks(mask):
    turned = mask.astype(F32).T
    side = turned.shape[0]
    return [
        jnp.broadcast_to(turned[:, r : r + 1], (side, 256)).astype(BF16)
        for r in range(turned.shape[1])
    ]


def edge_selector(rows, cols, picked):
    shape = (len(picked) * rows, rows * cols)
    out = lax.broadcasted_iota(jnp.int32, shape, 0)
    src = lax.broadcasted_iota(jnp.int32, shape, 1)
    want_row = out % rows
    want_col = picked[0] + out // rows
    return jnp.where(src == want_row * cols + want_col, 1.0, 0.0).astype(BF16)


def dot(a, b):
    return jnp.dot(a, b, preferred_element_type=F32)


def local_id(entry, slots):
    return jnp.where(entry < 0, -1, lax.rem(entry, slots))


def start_all(copies):
    for copy in copies:
        copy.start()
    return copies


def is_even():
    return lax.rem(lax.axis_index("tiles"), 2) == 0


def split_sides(west, east, across_ref, pair_ref):
    even = is_even()
    across_ref[...] = jnp.where(even, west, east).reshape(across_ref.shape)
    pair_ref[...] = jnp.where(even, east, west).reshape(pair_ref.shape)


def join_sides(across, pair):
    even = is_even()
    return jnp.where(even, across, pair), jnp.where(even, pair, across)


def load_kernel(
    x_hbm, cot_hbm, mask_hbm,
    across_ref, pair_ref, xe_ref, cote_ref, x_ref, cot_ref, ms,
    sems,
):
    slots, rows, cols, ch = x_ref.shape
    half = cols // 2
    mask_in = start_all([pltpu.make_async_copy(mask_hbm, ms, sems.at[0])])
    x_in, cot_in = (
        start_all(
            [
                pltpu.make_async_copy(src.at[s], dst.at[s], sems.at[1 + i * slots + s])
                for s in range(slots)
            ]
        )
        for i, (src, dst) in enumerate(((x_hbm, x_ref), (cot_hbm, cot_ref)))
    )
    sel = [
        edge_selector(rows, half, list(range(0, 4))),
        edge_selector(rows, half, list(range(half - 4, half))),
    ]
    mask_in[0].wait()
    oceans = {}
    for s in range(slots):
        mask = ms[s].astype(F32)
        for side in range(2):
            lo = 0 if side == 0 else cols - 4
            oceans[s, side] = jnp.stack(
                [
                    jnp.broadcast_to(mask[:, lo + k : lo + k + 1], (rows, ch)).astype(BF16)
                    for k in range(4)
                ]
            )
    for s in range(slots):
        x_in[s].wait()
        for side in range(2):
            tiles = slice(side * half, side * half + half)
            x = dot(sel[side], x_ref[s, :, tiles].reshape(rows * half, ch)).astype(BF16)
            xe_ref[s, side * 4 : side * 4 + 4] = x.reshape(4, rows, ch) * oceans[s, side]
    split_sides(xe_ref[:, 0:2], xe_ref[:, 6:8], across_ref, pair_ref)
    for s in range(slots):
        cot_in[s].wait()
        for side in range(2):
            tiles = slice(side * half, side * half + half)
            outer = slice(0, 2) if side == 0 else slice(2, 4)
            pick = sel[side][: 2 * rows] if side == 0 else sel[side][2 * rows :]
            c = dot(pick, cot_ref[s, :, tiles].reshape(rows * half, ch)).astype(BF16)
            cote_ref[side, s] = c.reshape(2, rows, ch) * oceans[s, side][outer]


def interior_kernel(
    own, nbr_ref, x_ref, cot_ref, w_ref, ms,
    out_ref, grad_ref, dw_ref, xc, gt,
    mk,
):
    slots, rows, cols, ch = x_ref.shape
    zeros = jnp.zeros((rows, STEP, ch), BF16)
    for s in range(slots):
        for r, line in enumerate(column_masks(ms[s])):
            mk[s, r] = line
    for s in range(slots):
        xm = x_ref[s] * mk[s]
        xc[s, STEP : rows + STEP, :, ch : 2 * ch] = xm
        xc[s, STEP : rows + STEP, :, 0:ch] = jnp.concatenate(
            [zeros, xm[:, : cols - STEP]], axis=1
        )
        xc[s, STEP : rows + STEP, :, 2 * ch :] = jnp.concatenate([xm[:, STEP:], zeros], axis=1)
    for s in range(slots):
        north, south = local_id(nbr_ref[s, 0], slots), local_id(nbr_ref[s, 1], slots)
        xc[s, 0:STEP] = xc[jnp.maximum(north, 0), rows : rows + STEP] * present_bf16(north)
        xc[s, rows + STEP :] = xc[jnp.maximum(south, 0), STEP : 2 * STEP] * present_bf16(south)

    block = 8
    column = lax.broadcasted_iota(jnp.int32, (block, cols, ch), 1)
    inside = jnp.where((column >= STEP) & (column < cols - STEP), 1.0, 0.0).astype(BF16)
    for s in range(slots):
        for r0 in range(0, rows, block):
            acc = None
            for a in range(3):
                window = xc[s, r0 + STEP * a : r0 + STEP * a + block].reshape(block * cols, 3 * ch)
                term = dot(window, w_ref[a])
                acc = term if acc is None else acc + term
            activated, derivative = gelu_pair(acc)
            ocean = mk[s, r0 : r0 + block]
            xm = xc[s, r0 + STEP : r0 + STEP + block, :, ch : 2 * ch].reshape(block * cols, ch)
            out = (xm.astype(F32) + activated).astype(BF16).reshape(block, cols, ch)
            out_ref[s, r0 : r0 + block] = out * ocean
            cot = (cot_ref[s, r0 : r0 + block] * ocean) * inside
            g = (cot.reshape(block * cols, ch).astype(F32) * derivative).astype(BF16)
            grad_ref[s, r0 : r0 + block] = g.reshape(block, cols, ch)
            turn_rows(gt.at[s], g, r0 * cols, own)

    rank = dw_ref.shape[0]
    place = 0 if own is None else other_half(rank)
    for a in range(3):
        dw_ref[:, a * 3 * ch : (a + 1) * 3 * ch] = tap_terms(gt, xc, a, place, rank)


def half_of(core, rank):
    return pl.multiple_of(core * rank, rank)


def own_half(rank):
    return half_of(lax.rem(lax.axis_index("tiles"), 2), rank)


def other_half(rank):
    return half_of(1 - lax.rem(lax.axis_index("tiles"), 2), rank)


def tap_terms(gt, xc, a, place, rank):
    slots, _, cells = gt.shape
    rows = xc.shape[1] - 2 * STEP
    wide = xc.shape[3]
    grads = [gt[s, pl.ds(place, rank), :] for s in range(slots)]
    windows = [xc[s, STEP * a : STEP * a + rows].reshape(cells, wide) for s in range(slots)]
    return dot(jnp.concatenate(grads, axis=1), jnp.concatenate(windows, axis=0))


def turn_rows(gt, g, first, own):
    turned = g.T
    ch, cells = turned.shape
    if own is None:
        gt[:, first : first + cells] = turned
        return
    for j in range(ch // own):
        to = (j % 2) * (ch // 2) + (j // 2) * own
        gt[to : to + own, first : first + cells] = turned[j * own : (j + 1) * own]


def stack_rows(own, north, south, entry_n, entry_s):
    rows = own.shape[1]
    above = north[:, rows - STEP :] * present_bf16(entry_n)
    below = south[:, :STEP] * present_bf16(entry_s)
    return jnp.concatenate([above, own, below], axis=1)


def edge_kernel(
    own, nbr_ref, across_ref, pair_ref, xe_ref, cote_ref, w_ref, dwi_ref,
    gacross_ref, gpair_ref, ge_ref, oe_ref, dw_ref, win, gt,
    sides,
):
    slots, _, rows, ch = xe_ref.shape
    sides[0], sides[1] = join_sides(across_ref[...], pair_ref[...])

    def local(s, column):
        return local_id(nbr_ref[s, column], slots)

    for s in range(slots):
        for side in range(2):
            for b in range(3):
                halo = (side == 0 and b == 0) or (side == 1 and b == 2)
                if halo:
                    src = sides.at[side]
                    mid, top, low = (2, 4, 6) if side == 0 else (3, 5, 7)
                    e_mid, e_top, e_low = local(s, mid), local(s, top), local(s, low)
                    middle = src[jnp.maximum(e_mid, 0)] * present_bf16(e_mid)
                    north = src[jnp.maximum(e_top, 0)]
                    south = src[jnp.maximum(e_low, 0)]
                else:
                    at = 2 * (b - 1) if side == 0 else 4 + 2 * b
                    e_top, e_low = local(s, 0), local(s, 1)
                    middle = xe_ref[s, at : at + 2]
                    north = xe_ref[jnp.maximum(e_top, 0), at : at + 2]
                    south = xe_ref[jnp.maximum(e_low, 0), at : at + 2]
                tall = stack_rows(middle, north, south, e_top, e_low)
                for a in range(3):
                    win[a, side, s, :, :, b * ch : (b + 1) * ch] = tall[
                        :, STEP * a : STEP * a + rows
                    ]
    cells = 2 * slots * 2 * rows
    acc = None
    for a in range(3):
        term = dot(win[a].reshape(cells, 3 * ch), w_ref[a])
        acc = term if acc is None else acc + term
    activated, derivative = gelu_pair(acc)
    x_own = win[1, :, :, :, :, ch : 2 * ch].reshape(cells, ch)
    oe_ref[...] = (x_own.astype(F32) + activated).astype(BF16).reshape(oe_ref.shape)
    g = (cote_ref[...].reshape(cells, ch).astype(F32) * derivative).astype(BF16)
    ge_ref[...] = g.reshape(ge_ref.shape)
    split_sides(g[: cells // 2], g[cells // 2 :], gacross_ref, gpair_ref)
    turn_rows(gt, g, 0, own)
    rank = dw_ref.shape[0]
    place = 0 if own is None else other_half(rank)
    turned = gt[pl.ds(place, rank), :]
    for a in range(3):
        span = slice(a * 3 * ch, (a + 1) * 3 * ch)
        total = dwi_ref[:, span] + dot(turned, win[a].reshape(cells, 3 * ch))
        dw_ref[:, span] = total.astype(dw_ref.dtype)


def keep_kernel(xc, gt, win, edge_gt, keep_ref):
    rank = keep_ref.shape[0]
    wide = xc.shape[3]
    place = own_half(rank)
    turned = edge_gt[pl.ds(place, rank), :]
    for a in range(3):
        edge = dot(turned, win[a].reshape(edge_gt.shape[1], wide))
        keep_ref[:, a * wide : (a + 1) * wide] = tap_terms(gt, xc, a, place, rank) + edge


def spread_selector(rows, cols, first):
    shape = (rows * cols, 2 * rows)
    out = lax.broadcasted_iota(jnp.int32, shape, 0)
    src = lax.broadcasted_iota(jnp.int32, shape, 1)
    want = (out % cols - first) * rows + out // cols
    return jnp.where((src == want) & (out % cols >= first) & (out % cols < first + 2), 1.0, 0.0).astype(BF16)


def input_grad_kernel(
    nbr_ref, gi_ref, oi_ref, ge_ref, oe_ref, across_ref, pair_ref, cot_ref, w_ref, mask_ref,
    out_hbm, ig_hbm,
    out_ref, ig_ref, gc, mk, hs, sems,
):
    slots, rows, cols, ch = gi_ref.shape
    half = cols // 2
    zeros = jnp.zeros((rows, STEP, ch), BF16)
    low = spread_selector(rows, half, 0)
    high = spread_selector(rows, half, half - 2)
    halos = join_sides(across_ref[...], pair_ref[...])

    def spread(sel, edge):
        return dot(sel, edge.reshape(2 * rows, ch)).astype(BF16).reshape(rows, half, ch)

    column = lax.broadcasted_iota(jnp.int32, (rows, half, ch), 1)
    for s in range(slots):
        for r, line in enumerate(column_masks(mask_ref[s])):
            mk[s, r] = line
        out_low = jnp.where(column < STEP, spread(low, oe_ref[0, s]), oi_ref[s, :, :half])
        out_ref[s, :, :half] = out_low * mk[s, :, :half]
        out_high = jnp.where(
            column >= half - STEP, spread(high, oe_ref[1, s]), oi_ref[s, :, half:]
        )
        out_ref[s, :, half:] = out_high * mk[s, :, half:]
        g = jnp.concatenate(
            [
                gi_ref[s, :, :half] + spread(low, ge_ref[0, s]),
                gi_ref[s, :, half:] + spread(high, ge_ref[1, s]),
            ],
            axis=1,
        )
        gc[s, STEP : rows + STEP, :, ch : 2 * ch] = g
        gc[s, STEP : rows + STEP, :, 2 * ch :] = jnp.concatenate(
            [zeros, g[:, : cols - STEP]], axis=1
        )
        gc[s, STEP : rows + STEP, :, 0:ch] = jnp.concatenate([g[:, STEP:], zeros], axis=1)
        hs[0, s] = spread(low, halos[0][s])
        hs[1, s] = spread(high, halos[1][s])
    stores = start_all(
        [pltpu.make_async_copy(out_ref.at[s], out_hbm.at[s], sems.at[s]) for s in range(slots)]
    )
    for s in range(slots):
        north, south = local_id(nbr_ref[s, 0], slots), local_id(nbr_ref[s, 1], slots)
        gc[s, 0:STEP] = gc[jnp.maximum(north, 0), rows : rows + STEP] * present_bf16(north)
        gc[s, rows + STEP :] = gc[jnp.maximum(south, 0), STEP : 2 * STEP] * present_bf16(south)
    for s in range(slots):
        for side, (mid, top, low_entry), lanes, lo in (
            (0, (2, 4, 6), 2 * ch, 0),
            (1, (3, 5, 7), 0, half),
        ):
            def piece(entry, first, count):
                entry = local_id(nbr_ref[s, entry], slots)
                return hs[side, jnp.maximum(entry, 0), first : first + count] * present_bf16(entry)

            halo = jnp.concatenate(
                [piece(top, rows - STEP, STEP), piece(mid, 0, rows), piece(low_entry, 0, STEP)],
                axis=0,
            )
            gc[s, :, lo : lo + half, lanes : lanes + ch] += halo
    block = 8
    for s in range(slots):
        for r0 in range(0, rows, block):
            acc = None
            for a in range(3):
                first = r0 + STEP * (2 - a)
                for b in range(3):
                    window = gc[s, first : first + block, :, b * ch : (b + 1) * ch].reshape(
                        block * cols, ch
                    )
                    term = lax.dot_general(
                        window,
                        w_ref[a, b * ch : (b + 1) * ch],
                        (((1,), (1,)), ((), ())),
                        preferred_element_type=F32,
                    )
                    acc = term if acc is None else acc + term
            cot = cot_ref[s, r0 : r0 + block].reshape(block * cols, ch).astype(F32)
            ig = (cot + acc).astype(BF16).reshape(block, cols, ch)
            ig_ref[s, r0 : r0 + block] = ig * mk[s, r0 : r0 + block]
        stores += start_all(
            [pltpu.make_async_copy(ig_ref.at[s], ig_hbm.at[s], sems.at[slots + s])]
        )
    for copy in stores:
        copy.wait()


def permute(value, pairs_of):
    count = lax.axis_size("tiles")
    return lax.ppermute(value, "tiles", [(i, pairs_of(i, count)) for i in range(count)])


def swap_halos(across, pair):
    across = permute(across, lambda i, n: (i - 1 if i % 2 == 0 else i + 1) % n)
    return across, permute(pair, lambda i, n: i ^ 1)


def stage_sizes(count):
    rest = count // 2
    middle = 1
    while middle * middle * 4 <= rest:
        middle *= 2
    return rest // middle, middle, 2


def exchange_sum(total, axis, position, size, stride):
    acc = lax.dynamic_index_in_dim(total, position, axis, False)
    parts = []
    for k in range(1, size):
        other = lax.dynamic_index_in_dim(total, position ^ k, axis, False).astype(BF16)
        parts.append(permute(other, lambda i, n: i ^ (k * stride)))
    for part in parts:
        acc = acc + part.astype(F32)
    return acc


def scatter_sum(dw, device):
    count = lax.axis_size("tiles")
    outer, middle, core = stage_sizes(count)
    own_rows = dw.shape[0] // count
    total = dw.reshape(outer, middle, core, own_rows, dw.shape[1])
    c, y, z = device % core, device // core % middle, device // (core * middle)
    total = exchange_sum(total, 2, c, core, 1)
    total = exchange_sum(total, 1, y, middle, core)
    return exchange_sum(total, 0, z, outer, core * middle)


def split_kernel(stride, keep_ref, *refs):
    size = keep_ref.shape[1]
    count = len(refs) - size
    recvs, keep_out, sends = refs[:count], refs[count], refs[count + 1 :]
    place = lax.rem(lax.axis_index("tiles") // stride, size)
    for i in range(keep_ref.shape[0]):
        for k in range(size):
            acc = keep_ref[i, place ^ k]
            for recv in recvs:
                acc = acc + recv[i, place ^ k].astype(F32)
            if k == 0:
                keep_out[i] = acc
            else:
                sends[k - 1][i] = acc.astype(BF16)


def last_kernel(scale, keep_ref, *refs):
    *recvs, out_ref = refs
    acc = keep_ref[...]
    for recv in recvs:
        acc = acc + recv[...].astype(F32)
    out_ref[...] = acc * scale


def small_call(kernel, out_shapes, name, *args):
    return pl.pallas_call(
        kernel,
        out_shape=out_shapes,
        in_specs=[VMEM] * len(args),
        out_specs=tuple(VMEM for _ in out_shapes),
        compiler_params=pltpu.CompilerParams(vmem_limit_bytes=8 << 20),
        name=name,
    )(*args)


def shape_f32(*dims):
    return jax.ShapeDtypeStruct(dims, F32)


def shape_bf16(*dims):
    return jax.ShapeDtypeStruct(dims, BF16)


def shards(input_field, cotangent, weight, neighbours, land_mask):
    device = lax.axis_index("tiles")
    count = lax.axis_size("tiles")
    slots, rows, cols, ch = input_field.shape
    taps = weight.reshape(3, 3 * ch, ch)
    params = pltpu.CompilerParams(vmem_limit_bytes=VMEM_BYTES)
    side_columns = (slots, STEP, rows, ch)
    field = input_field.shape
    own = ch // count if ch // count % 16 == 0 else None
    outer, middle, _ = stage_sizes(count)

    across, pair, x_edge, cot_edge, field_in, cot_in, ocean = pl.pallas_call(
        load_kernel,
        out_shape=(
            shape_bf16(*side_columns),
            shape_bf16(*side_columns),
            shape_bf16(slots, 8, rows, ch),
            shape_bf16(2, *side_columns),
            shape_bf16(*field),
            shape_bf16(*field),
            jax.ShapeDtypeStruct(land_mask.shape, jnp.int32),
        ),
        in_specs=[HBM] * 3,
        out_specs=(VMEM,) * 7,
        scratch_shapes=[pltpu.SemaphoreType.DMA((1 + 2 * slots,))],
        compiler_params=pltpu.CompilerParams(vmem_limit_bytes=LOAD_BYTES),
        name="load",
    )(input_field, cotangent, land_mask)
    across, pair = swap_halos(across, pair)

    rank = ch if own is None else ch // 2
    out_inner, grad_inner, dw_inner, windows, turned = pl.pallas_call(
        functools.partial(interior_kernel, own),
        out_shape=(
            shape_bf16(*field),
            shape_bf16(*field),
            shape_f32(rank, 9 * ch),
            shape_bf16(slots, rows + 2 * STEP, cols, 3 * ch),
            shape_bf16(slots, ch, rows * cols),
        ),
        in_specs=[SMEM] + [VMEM] * 4,
        out_specs=(VMEM,) * 5,
        scratch_shapes=[pltpu.VMEM(field, BF16)],
        compiler_params=params,
        cost_estimate=pl.CostEstimate(
            flops=4 * 9 * slots * rows * cols * ch * ch, bytes_accessed=8 << 20, transcendentals=0
        ),
        name="interior",
    )(neighbours, field_in, cot_in, taps, ocean)

    grad_across, grad_pair, grad_edge, out_edge, dw, edge_windows, edge_turned = pl.pallas_call(
        functools.partial(edge_kernel, own),
        out_shape=(
            shape_bf16(*side_columns),
            shape_bf16(*side_columns),
            shape_bf16(2, *side_columns),
            shape_bf16(2, *side_columns),
            shape_f32(ch, 9 * ch) if own is None else shape_bf16(rank, 9 * ch),
            shape_bf16(3, 2, slots, STEP, rows, 3 * ch),
            shape_bf16(ch, 4 * slots * rows),
        ),
        in_specs=[SMEM] + [VMEM] * 6,
        out_specs=(VMEM,) * 7,
        scratch_shapes=[pltpu.VMEM((2, *side_columns), BF16)],
        compiler_params=params,
        cost_estimate=pl.CostEstimate(
            flops=4 * 9 * slots * rows * 4 * ch * ch, bytes_accessed=6 << 20, transcendentals=0
        ),
        name="edges",
    )(neighbours, across, pair, x_edge, cot_edge, taps, dw_inner)

    grad_across, grad_pair = swap_halos(grad_across, grad_pair)

    def input_grad_call(grad_edge):
        return pl.pallas_call(
            input_grad_kernel,
            out_shape=(shape_bf16(*field), shape_bf16(*field)),
            in_specs=[SMEM] + [VMEM] * 9,
            out_specs=(HBM, HBM),
            scratch_shapes=[pltpu.VMEM(field, BF16)] * 2
            + [
                pltpu.VMEM((slots, rows + 2 * STEP, cols, 3 * ch), BF16),
                pltpu.VMEM(field, BF16),
                pltpu.VMEM((2, slots, rows, cols // 2, ch), BF16),
                pltpu.SemaphoreType.DMA((2 * slots,)),
            ],
            compiler_params=params,
            cost_estimate=pl.CostEstimate(
                flops=2 * 9 * slots * rows * cols * ch * ch,
                bytes_accessed=8 << 20,
                transcendentals=0,
            ),
            name="input_grad",
        )(
            neighbours, grad_inner, out_inner, grad_edge, out_edge,
            grad_across, grad_pair, cot_in, taps, ocean,
        )

    scale_factor = 1.0 / (rows * math.sqrt(slots * count))
    if own is None:
        summed = scatter_sum(dw, device)
        return *input_grad_call(grad_edge), summed * scale_factor

    wide = 9 * ch
    recv = permute(dw, lambda i, n: i ^ 1)
    (keep,) = pl.pallas_call(
        keep_kernel,
        out_shape=(shape_f32(rank, wide),),
        in_specs=[VMEM] * 4,
        out_specs=(VMEM,),
        compiler_params=params,
        cost_estimate=pl.CostEstimate(
            flops=9 * slots * rows * (cols + 4) * ch * ch, bytes_accessed=0, transcendentals=0
        ),
        name="keep",
    )(windows, turned, edge_windows, edge_turned)
    whole = (outer, middle, own, wide)
    keep, *sends = small_call(
        functools.partial(split_kernel, 2),
        (shape_f32(outer, own, wide), *[shape_bf16(outer, own, wide)] * (middle - 1)),
        "middle_terms", keep.reshape(whole), recv.reshape(whole),
    )
    recvs = [permute(sends[k - 1], lambda i, n, k=k: i ^ (k * 2)) for k in range(1, middle)]
    keep, *sends = small_call(
        functools.partial(split_kernel, 2 * middle),
        (shape_f32(1, own, wide), *[shape_bf16(1, own, wide)] * (outer - 1)),
        "outer_terms", keep[None], *[recv[None] for recv in recvs],
    )
    keep, grad_edge = lax.optimization_barrier((keep, grad_edge))
    recvs = [
        permute(sends[k - 1], lambda i, n, k=k: i ^ (k * 2 * middle))
        for k in reversed(range(1, outer))
    ]
    layer_output, input_grad = input_grad_call(grad_edge)
    (summed,) = small_call(
        functools.partial(last_kernel, scale_factor),
        (shape_f32(1, own, wide),),
        "last_sum", keep, *recvs,
    )
    return layer_output, input_grad, summed[0]


def solution(mesh):
    return jax.shard_map(
        shards,
        mesh=mesh,
        in_specs=(
            P(("groups", "tiles"), None, None, None),
            P(("groups", "tiles"), None, None, None),
            P(),
            P("tiles", None),
            P("tiles", None, None),
        ),
        out_specs=(
            P(("groups", "tiles"), None, None, None),
            P(("groups", "tiles"), None, None, None),
            P(("groups", "tiles"), None),
        ),
        check_vma=False,
    )
```

```python
import functools
import math

import jax
import jax.numpy as jnp
from jax import lax
from jax.experimental import pallas as pl
from jax.experimental.pallas import tpu as pltpu
from jax.sharding import PartitionSpec as P

STEP = 2
BF16 = jnp.bfloat16
F32 = jnp.float32
GELU_SCALE = math.sqrt(2.0 / math.pi)
GELU_CUBIC = 0.044715
VMEM_BYTES = 16 << 20
LOAD_BYTES = 101 << 19

SMEM = pl.BlockSpec(memory_space=pltpu.SMEM)
VMEM = pl.BlockSpec(memory_space=pltpu.VMEM)
HBM = pl.BlockSpec(memory_space=pltpu.HBM)


def gelu_pair(h):
    h2 = h * h
    t = jnp.tanh(h * (GELU_SCALE + (GELU_SCALE * GELU_CUBIC) * h2))
    half_up = 0.5 + 0.5 * t
    activated = h * half_up
    derivative = half_up + h * (0.5 - 0.5 * t * t) * (
        GELU_SCALE + (3.0 * GELU_CUBIC * GELU_SCALE) * h2
    )
    return activated, derivative


def present_bf16(entry):
    return jnp.where(entry >= 0, 1.0, 0.0).astype(BF16)


def column_masks(mask):
    turned = mask.astype(F32).T
    side = turned.shape[0]
    return [
        jnp.broadcast_to(turned[:, r : r + 1], (side, 256)).astype(BF16)
        for r in range(turned.shape[1])
    ]


def edge_selector(rows, cols, picked):
    shape = (len(picked) * rows, rows * cols)
    out = lax.broadcasted_iota(jnp.int32, shape, 0)
    src = lax.broadcasted_iota(jnp.int32, shape, 1)
    want_row = out % rows
    want_col = picked[0] + out // rows
    return jnp.where(src == want_row * cols + want_col, 1.0, 0.0).astype(BF16)


def dot(a, b):
    return jnp.dot(a, b, preferred_element_type=F32)


def local_id(entry, slots):
    return jnp.where(entry < 0, -1, lax.rem(entry, slots))


def start_all(copies):
    for copy in copies:
        copy.start()
    return copies


def is_even():
    return lax.rem(lax.axis_index("tiles"), 2) == 0


def split_sides(west, east, across_ref, pair_ref):
    even = is_even()
    across_ref[...] = jnp.where(even, west, east).reshape(across_ref.shape)
    pair_ref[...] = jnp.where(even, east, west).reshape(pair_ref.shape)


def join_sides(across, pair):
    even = is_even()
    return jnp.where(even, across, pair), jnp.where(even, pair, across)


def load_kernel(
    x_hbm, cot_hbm, mask_hbm,
    across_ref, pair_ref, xe_ref, cote_ref, x_ref, cot_ref, ms,
    sems,
):
    slots, rows, cols, ch = x_ref.shape
    half = cols // 2
    mask_in = start_all([pltpu.make_async_copy(mask_hbm, ms, sems.at[0])])
    x_in, cot_in = (
        start_all(
            [
                pltpu.make_async_copy(src.at[s], dst.at[s], sems.at[1 + i * slots + s])
                for s in range(slots)
            ]
        )
        for i, (src, dst) in enumerate(((x_hbm, x_ref), (cot_hbm, cot_ref)))
    )
    sel = [
        edge_selector(rows, half, list(range(0, 4))),
        edge_selector(rows, half, list(range(half - 4, half))),
    ]
    mask_in[0].wait()
    oceans = {}
    for s in range(slots):
        mask = ms[s].astype(F32)
        for side in range(2):
            lo = 0 if side == 0 else cols - 4
            oceans[s, side] = jnp.stack(
                [
                    jnp.broadcast_to(mask[:, lo + k : lo + k + 1], (rows, ch)).astype(BF16)
                    for k in range(4)
                ]
            )
    for s in range(slots):
        x_in[s].wait()
        for side in range(2):
            tiles = slice(side * half, side * half + half)
            x = dot(sel[side], x_ref[s, :, tiles].reshape(rows * half, ch)).astype(BF16)
            xe_ref[s, side * 4 : side * 4 + 4] = x.reshape(4, rows, ch) * oceans[s, side]
    split_sides(xe_ref[:, 0:2], xe_ref[:, 6:8], across_ref, pair_ref)
    for s in range(slots):
        cot_in[s].wait()
        for side in range(2):
            tiles = slice(side * half, side * half + half)
            outer = slice(0, 2) if side == 0 else slice(2, 4)
            pick = sel[side][: 2 * rows] if side == 0 else sel[side][2 * rows :]
            c = dot(pick, cot_ref[s, :, tiles].reshape(rows * half, ch)).astype(BF16)
            cote_ref[side, s] = c.reshape(2, rows, ch) * oceans[s, side][outer]


def interior_kernel(
    own, nbr_ref, x_ref, cot_ref, w_ref, ms,
    out_ref, grad_ref, dw_ref, xc, gt,
    mk,
):
    slots, rows, cols, ch = x_ref.shape
    zeros = jnp.zeros((rows, STEP, ch), BF16)
    for s in range(slots):
        for r, line in enumerate(column_masks(ms[s])):
            mk[s, r] = line
    for s in range(slots):
        xm = x_ref[s] * mk[s]
        xc[s, STEP : rows + STEP, :, ch : 2 * ch] = xm
        xc[s, STEP : rows + STEP, :, 0:ch] = jnp.concatenate(
            [zeros, xm[:, : cols - STEP]], axis=1
        )
        xc[s, STEP : rows + STEP, :, 2 * ch :] = jnp.concatenate([xm[:, STEP:], zeros], axis=1)
    for s in range(slots):
        north, south = local_id(nbr_ref[s, 0], slots), local_id(nbr_ref[s, 1], slots)
        xc[s, 0:STEP] = xc[jnp.maximum(north, 0), rows : rows + STEP] * present_bf16(north)
        xc[s, rows + STEP :] = xc[jnp.maximum(south, 0), STEP : 2 * STEP] * present_bf16(south)

    block = 8
    column = lax.broadcasted_iota(jnp.int32, (block, cols, ch), 1)
    inside = jnp.where((column >= STEP) & (column < cols - STEP), 1.0, 0.0).astype(BF16)
    for s in range(slots):
        for r0 in range(0, rows, block):
            acc = None
            for a in range(3):
                window = xc[s, r0 + STEP * a : r0 + STEP * a + block].reshape(block * cols, 3 * ch)
                term = dot(window, w_ref[a])
                acc = term if acc is None else acc + term
            activated, derivative = gelu_pair(acc)
            ocean = mk[s, r0 : r0 + block]
            xm = xc[s, r0 + STEP : r0 + STEP + block, :, ch : 2 * ch].reshape(block * cols, ch)
            out = (xm.astype(F32) + activated).astype(BF16).reshape(block, cols, ch)
            out_ref[s, r0 : r0 + block] = out * ocean
            cot = (cot_ref[s, r0 : r0 + block] * ocean) * inside
            g = (cot.reshape(block * cols, ch).astype(F32) * derivative).astype(BF16)
            grad_ref[s, r0 : r0 + block] = g.reshape(block, cols, ch)
            turn_rows(gt.at[s], g, r0 * cols, own)

    rank = dw_ref.shape[0]
    place = 0 if own is None else other_half(rank)
    for a in range(3):
        dw_ref[:, a * 3 * ch : (a + 1) * 3 * ch] = tap_terms(gt, xc, a, place, rank)


def half_of(core, rank):
    return pl.multiple_of(core * rank, rank)


def own_half(rank):
    return half_of(lax.rem(lax.axis_index("tiles"), 2), rank)


def other_half(rank):
    return half_of(1 - lax.rem(lax.axis_index("tiles"), 2), rank)


def tap_terms(gt, xc, a, place, rank):
    slots, _, cells = gt.shape
    rows = xc.shape[1] - 2 * STEP
    wide = xc.shape[3]
    grads = [gt[s, pl.ds(place, rank), :] for s in range(slots)]
    windows = [xc[s, STEP * a : STEP * a + rows].reshape(cells, wide) for s in range(slots)]
    return dot(jnp.concatenate(grads, axis=1), jnp.concatenate(windows, axis=0))


def turn_rows(gt, g, first, own):
    turned = g.T
    ch, cells = turned.shape
    if own is None:
        gt[:, first : first + cells] = turned
        return
    for j in range(ch // own):
        to = (j % 2) * (ch // 2) + (j // 2) * own
        gt[to : to + own, first : first + cells] = turned[j * own : (j + 1) * own]


def stack_rows(own, north, south, entry_n, entry_s):
    rows = own.shape[1]
    above = north[:, rows - STEP :] * present_bf16(entry_n)
    below = south[:, :STEP] * present_bf16(entry_s)
    return jnp.concatenate([above, own, below], axis=1)


def edge_kernel(
    own, nbr_ref, across_ref, pair_ref, xe_ref, cote_ref, w_ref, dwi_ref,
    gacross_ref, gpair_ref, ge_ref, oe_ref, dw_ref, win, gt,
    sides,
):
    slots, _, rows, ch = xe_ref.shape
    sides[0], sides[1] = join_sides(across_ref[...], pair_ref[...])

    def local(s, column):
        return local_id(nbr_ref[s, column], slots)

    for s in range(slots):
        for side in range(2):
            for b in range(3):
                halo = (side == 0 and b == 0) or (side == 1 and b == 2)
                if halo:
                    src = sides.at[side]
                    mid, top, low = (2, 4, 6) if side == 0 else (3, 5, 7)
                    e_mid, e_top, e_low = local(s, mid), local(s, top), local(s, low)
                    middle = src[jnp.maximum(e_mid, 0)] * present_bf16(e_mid)
                    north = src[jnp.maximum(e_top, 0)]
                    south = src[jnp.maximum(e_low, 0)]
                else:
                    at = 2 * (b - 1) if side == 0 else 4 + 2 * b
                    e_top, e_low = local(s, 0), local(s, 1)
                    middle = xe_ref[s, at : at + 2]
                    north = xe_ref[jnp.maximum(e_top, 0), at : at + 2]
                    south = xe_ref[jnp.maximum(e_low, 0), at : at + 2]
                tall = stack_rows(middle, north, south, e_top, e_low)
                for a in range(3):
                    win[a, side, s, :, :, b * ch : (b + 1) * ch] = tall[
                        :, STEP * a : STEP * a + rows
                    ]
    cells = 2 * slots * 2 * rows
    acc = None
    for a in range(3):
        term = dot(win[a].reshape(cells, 3 * ch), w_ref[a])
        acc = term if acc is None else acc + term
    activated, derivative = gelu_pair(acc)
    x_own = win[1, :, :, :, :, ch : 2 * ch].reshape(cells, ch)
    oe_ref[...] = (x_own.astype(F32) + activated).astype(BF16).reshape(oe_ref.shape)
    g = (cote_ref[...].reshape(cells, ch).astype(F32) * derivative).astype(BF16)
    ge_ref[...] = g.reshape(ge_ref.shape)
    split_sides(g[: cells // 2], g[cells // 2 :], gacross_ref, gpair_ref)
    turn_rows(gt, g, 0, own)
    rank = dw_ref.shape[0]
    place = 0 if own is None else other_half(rank)
    turned = gt[pl.ds(place, rank), :]
    for a in range(3):
        span = slice(a * 3 * ch, (a + 1) * 3 * ch)
        total = dwi_ref[:, span] + dot(turned, win[a].reshape(cells, 3 * ch))
        dw_ref[:, span] = total.astype(dw_ref.dtype)


def keep_kernel(xc, gt, win, edge_gt, keep_ref):
    rank = keep_ref.shape[0]
    wide = xc.shape[3]
    place = own_half(rank)
    turned = edge_gt[pl.ds(place, rank), :]
    for a in range(3):
        edge = dot(turned, win[a].reshape(edge_gt.shape[1], wide))
        keep_ref[:, a * wide : (a + 1) * wide] = tap_terms(gt, xc, a, place, rank) + edge


def spread_selector(rows, cols, first):
    shape = (rows * cols, 2 * rows)
    out = lax.broadcasted_iota(jnp.int32, shape, 0)
    src = lax.broadcasted_iota(jnp.int32, shape, 1)
    want = (out % cols - first) * rows + out // cols
    return jnp.where((src == want) & (out % cols >= first) & (out % cols < first + 2), 1.0, 0.0).astype(BF16)


def spread_edge(sel, edge):
    _, rows, ch = edge.shape
    return dot(sel, edge.reshape(2 * rows, ch)).astype(BF16).reshape(rows, -1, ch)


def gradient_kernel(
    nbr_ref, gi_ref, oi_ref, ge_ref, oe_ref, mask_ref, w_ref,
    out_hbm, gc, mk, wt_ref,
    out_ref, sems,
):
    slots, rows, cols, ch = gi_ref.shape
    half = cols // 2
    zeros = jnp.zeros((rows, STEP, ch), BF16)
    low = spread_selector(rows, half, 0)
    high = spread_selector(rows, half, half - 2)
    column = lax.broadcasted_iota(jnp.int32, (rows, half, ch), 1)
    stores = []
    for s in range(slots):
        for r, line in enumerate(column_masks(mask_ref[s])):
            mk[s, r] = line
        out_low = jnp.where(column < STEP, spread_edge(low, oe_ref[0, s]), oi_ref[s, :, :half])
        out_ref[s, :, :half] = out_low * mk[s, :, :half]
        out_high = jnp.where(
            column >= half - STEP, spread_edge(high, oe_ref[1, s]), oi_ref[s, :, half:]
        )
        out_ref[s, :, half:] = out_high * mk[s, :, half:]
        stores += start_all([pltpu.make_async_copy(out_ref.at[s], out_hbm.at[s], sems.at[s])])
    for s in range(slots):
        g = jnp.concatenate(
            [
                gi_ref[s, :, :half] + spread_edge(low, ge_ref[0, s]),
                gi_ref[s, :, half:] + spread_edge(high, ge_ref[1, s]),
            ],
            axis=1,
        )
        gc[s, STEP : rows + STEP, :, ch : 2 * ch] = g
        gc[s, STEP : rows + STEP, :, 2 * ch :] = jnp.concatenate(
            [zeros, g[:, : cols - STEP]], axis=1
        )
        gc[s, STEP : rows + STEP, :, 0:ch] = jnp.concatenate([g[:, STEP:], zeros], axis=1)
    for s in range(slots):
        north, south = local_id(nbr_ref[s, 0], slots), local_id(nbr_ref[s, 1], slots)
        gc[s, 0:STEP] = gc[jnp.maximum(north, 0), rows : rows + STEP] * present_bf16(north)
        gc[s, rows + STEP :] = gc[jnp.maximum(south, 0), STEP : 2 * STEP] * present_bf16(south)
    for a in range(3):
        for b in range(3):
            lanes = slice(b * ch, (b + 1) * ch)
            wt_ref[a, lanes] = w_ref[a, lanes].T
    for copy in stores:
        copy.wait()


def input_grad_kernel(
    nbr_ref, gc, mk, across_ref, pair_ref, cot_ref, wt_ref,
    ig_hbm,
    ig_ref, hs, ht, sems,
):
    slots, rows, cols, ch = cot_ref.shape
    half = cols // 2
    halos = join_sides(across_ref[...], pair_ref[...])
    for side in range(2):
        sel = spread_selector(rows, half, 0 if side == 0 else half - 2)
        for s in range(slots):
            hs[side, s] = spread_edge(sel, halos[side][s])
    for s in range(slots):
        for side, entries in enumerate(((4, 2, 6), (5, 3, 7))):
            lo, lanes = (0, 2 * ch) if side == 0 else (half, 0)
            for column, span, at in zip(
                entries,
                (slice(rows - STEP, rows), slice(0, rows), slice(0, STEP)),
                (slice(0, STEP), slice(STEP, rows + STEP), slice(rows + STEP, None)),
            ):
                entry = local_id(nbr_ref[s, column], slots)
                halo = hs[side, jnp.maximum(entry, 0), span] * present_bf16(entry)
                ht[side, s, at] = gc[s, at, lo : lo + half, lanes : lanes + ch] + halo
    block = 8
    stores = []
    for s in range(slots):
        for r0 in range(0, rows, block):
            acc = None
            for a in range(3):
                at = slice(r0 + STEP * (2 - a), r0 + STEP * (2 - a) + block)
                window = jnp.concatenate(
                    [
                        jnp.concatenate([gc[s, at, :half, :ch], ht[1, s, at]], axis=1),
                        gc[s, at, :, ch : 2 * ch],
                        jnp.concatenate([ht[0, s, at], gc[s, at, half:, 2 * ch :]], axis=1),
                    ],
                    axis=2,
                )
                term = dot(window.reshape(block * cols, 3 * ch), wt_ref[a])
                acc = term if acc is None else acc + term
            cot = cot_ref[s, r0 : r0 + block].reshape(block * cols, ch).astype(F32)
            ig = (cot + acc).astype(BF16).reshape(block, cols, ch)
            ig_ref[s, r0 : r0 + block] = ig * mk[s, r0 : r0 + block]
        stores += start_all([pltpu.make_async_copy(ig_ref.at[s], ig_hbm.at[s], sems.at[s])])
    for copy in stores:
        copy.wait()


def permute(value, pairs_of):
    count = lax.axis_size("tiles")
    return lax.ppermute(value, "tiles", [(i, pairs_of(i, count)) for i in range(count)])


def swap_halos(across, pair):
    across = permute(across, lambda i, n: (i - 1 if i % 2 == 0 else i + 1) % n)
    return across, permute(pair, lambda i, n: i ^ 1)


def stage_sizes(count):
    rest = count // 2
    middle = 1
    while middle * middle * 4 <= rest:
        middle *= 2
    return rest // middle, middle, 2


def exchange_sum(total, axis, position, size, stride):
    acc = lax.dynamic_index_in_dim(total, position, axis, False)
    parts = []
    for k in range(1, size):
        other = lax.dynamic_index_in_dim(total, position ^ k, axis, False).astype(BF16)
        parts.append(permute(other, lambda i, n: i ^ (k * stride)))
    for part in parts:
        acc = acc + part.astype(F32)
    return acc


def scatter_sum(dw, device):
    count = lax.axis_size("tiles")
    outer, middle, core = stage_sizes(count)
    own_rows = dw.shape[0] // count
    total = dw.reshape(outer, middle, core, own_rows, dw.shape[1])
    c, y, z = device % core, device // core % middle, device // (core * middle)
    total = exchange_sum(total, 2, c, core, 1)
    total = exchange_sum(total, 1, y, middle, core)
    return exchange_sum(total, 0, z, outer, core * middle)


def split_kernel(stride, keep_ref, *refs):
    size = keep_ref.shape[1]
    count = len(refs) - size
    recvs, keep_out, sends = refs[:count], refs[count], refs[count + 1 :]
    place = lax.rem(lax.axis_index("tiles") // stride, size)
    for i in range(keep_ref.shape[0]):
        for k in range(size):
            acc = keep_ref[i, place ^ k]
            for recv in recvs:
                acc = acc + recv[i, place ^ k].astype(F32)
            if k == 0:
                keep_out[i] = acc
            else:
                sends[k - 1][i] = acc.astype(BF16)


def last_kernel(scale, keep_ref, *refs):
    *recvs, out_ref = refs
    acc = keep_ref[...]
    for recv in recvs:
        acc = acc + recv[...].astype(F32)
    out_ref[...] = acc * scale


def small_call(kernel, out_shapes, name, *args):
    return pl.pallas_call(
        kernel,
        out_shape=out_shapes,
        in_specs=[VMEM] * len(args),
        out_specs=tuple(VMEM for _ in out_shapes),
        compiler_params=pltpu.CompilerParams(vmem_limit_bytes=8 << 20),
        name=name,
    )(*args)


def shape_f32(*dims):
    return jax.ShapeDtypeStruct(dims, F32)


def shape_bf16(*dims):
    return jax.ShapeDtypeStruct(dims, BF16)


def shards(input_field, cotangent, weight, neighbours, land_mask):
    device = lax.axis_index("tiles")
    count = lax.axis_size("tiles")
    slots, rows, cols, ch = input_field.shape
    taps = weight.reshape(3, 3 * ch, ch)
    params = pltpu.CompilerParams(vmem_limit_bytes=VMEM_BYTES)
    side_columns = (slots, STEP, rows, ch)
    field = input_field.shape
    own = ch // count if ch // count % 16 == 0 else None
    outer, middle, _ = stage_sizes(count)

    across, pair, x_edge, cot_edge, field_in, cot_in, ocean = pl.pallas_call(
        load_kernel,
        out_shape=(
            shape_bf16(*side_columns),
            shape_bf16(*side_columns),
            shape_bf16(slots, 8, rows, ch),
            shape_bf16(2, *side_columns),
            shape_bf16(*field),
            shape_bf16(*field),
            jax.ShapeDtypeStruct(land_mask.shape, jnp.int32),
        ),
        in_specs=[HBM] * 3,
        out_specs=(VMEM,) * 7,
        scratch_shapes=[pltpu.SemaphoreType.DMA((1 + 2 * slots,))],
        compiler_params=pltpu.CompilerParams(vmem_limit_bytes=LOAD_BYTES),
        name="load",
    )(input_field, cotangent, land_mask)
    across, pair = swap_halos(across, pair)

    rank = ch if own is None else ch // 2
    out_inner, grad_inner, dw_inner, windows, turned = pl.pallas_call(
        functools.partial(interior_kernel, own),
        out_shape=(
            shape_bf16(*field),
            shape_bf16(*field),
            shape_f32(rank, 9 * ch),
            shape_bf16(slots, rows + 2 * STEP, cols, 3 * ch),
            shape_bf16(slots, ch, rows * cols),
        ),
        in_specs=[SMEM] + [VMEM] * 4,
        out_specs=(VMEM,) * 5,
        scratch_shapes=[pltpu.VMEM(field, BF16)],
        compiler_params=params,
        cost_estimate=pl.CostEstimate(
            flops=4 * 9 * slots * rows * cols * ch * ch, bytes_accessed=8 << 20, transcendentals=0
        ),
        name="interior",
    )(neighbours, field_in, cot_in, taps, ocean)

    grad_across, grad_pair, grad_edge, out_edge, dw, edge_windows, edge_turned = pl.pallas_call(
        functools.partial(edge_kernel, own),
        out_shape=(
            shape_bf16(*side_columns),
            shape_bf16(*side_columns),
            shape_bf16(2, *side_columns),
            shape_bf16(2, *side_columns),
            shape_f32(ch, 9 * ch) if own is None else shape_bf16(rank, 9 * ch),
            shape_bf16(3, 2, slots, STEP, rows, 3 * ch),
            shape_bf16(ch, 4 * slots * rows),
        ),
        in_specs=[SMEM] + [VMEM] * 6,
        out_specs=(VMEM,) * 7,
        scratch_shapes=[pltpu.VMEM((2, *side_columns), BF16)],
        compiler_params=params,
        cost_estimate=pl.CostEstimate(
            flops=4 * 9 * slots * rows * 4 * ch * ch, bytes_accessed=6 << 20, transcendentals=0
        ),
        name="edges",
    )(neighbours, across, pair, x_edge, cot_edge, taps, dw_inner)

    grad_across, grad_pair = swap_halos(grad_across, grad_pair)

    def gradient_call(grad_edge):
        return pl.pallas_call(
            gradient_kernel,
            out_shape=(
                shape_bf16(*field),
                shape_bf16(slots, rows + 2 * STEP, cols, 3 * ch),
                shape_bf16(*field),
                shape_bf16(3, 3 * ch, ch),
            ),
            in_specs=[SMEM] + [VMEM] * 6,
            out_specs=(HBM, VMEM, VMEM, VMEM),
            scratch_shapes=[pltpu.VMEM(field, BF16), pltpu.SemaphoreType.DMA((slots,))],
            compiler_params=params,
            cost_estimate=pl.CostEstimate(flops=1 << 31, bytes_accessed=0, transcendentals=0),
            name="gradient",
        )(neighbours, grad_inner, out_inner, grad_edge, out_edge, ocean, taps)

    def input_grad_call(shifted, masks, turned_taps):
        return pl.pallas_call(
            input_grad_kernel,
            out_shape=shape_bf16(*field),
            in_specs=[SMEM] + [VMEM] * 6,
            out_specs=HBM,
            scratch_shapes=[
                pltpu.VMEM(field, BF16),
                pltpu.VMEM((2, slots, rows, cols // 2, ch), BF16),
                pltpu.VMEM((2, slots, rows + 2 * STEP, cols // 2, ch), BF16),
                pltpu.SemaphoreType.DMA((slots,)),
            ],
            compiler_params=params,
            cost_estimate=pl.CostEstimate(
                flops=2 * 9 * slots * rows * cols * ch * ch,
                bytes_accessed=8 << 20,
                transcendentals=0,
            ),
            name="input_grad",
        )(neighbours, shifted, masks, grad_across, grad_pair, cot_in, turned_taps)

    scale_factor = 1.0 / (rows * math.sqrt(slots * count))
    if own is None:
        summed = scatter_sum(dw, device)
        layer_output, shifted, masks, turned_taps = gradient_call(grad_edge)
        return layer_output, input_grad_call(shifted, masks, turned_taps), summed * scale_factor

    wide = 9 * ch
    recv = permute(dw, lambda i, n: i ^ 1)
    (keep,) = pl.pallas_call(
        keep_kernel,
        out_shape=(shape_f32(rank, wide),),
        in_specs=[VMEM] * 4,
        out_specs=(VMEM,),
        compiler_params=params,
        cost_estimate=pl.CostEstimate(
            flops=9 * slots * rows * (cols + 4) * ch * ch, bytes_accessed=0, transcendentals=0
        ),
        name="keep",
    )(windows, turned, edge_windows, edge_turned)
    whole = (outer, middle, own, wide)
    keep, *sends = small_call(
        functools.partial(split_kernel, 2),
        (shape_f32(outer, own, wide), *[shape_bf16(outer, own, wide)] * (middle - 1)),
        "middle_terms", keep.reshape(whole), recv.reshape(whole),
    )
    recvs = [permute(sends[k - 1], lambda i, n, k=k: i ^ (k * 2)) for k in range(1, middle)]
    keep, grad_edge = lax.optimization_barrier((keep, grad_edge))
    layer_output, shifted, masks, turned_taps = gradient_call(grad_edge)
    keep, *recvs, shifted = lax.optimization_barrier((keep, *recvs, shifted))
    keep, *sends = small_call(
        functools.partial(split_kernel, 2 * middle),
        (shape_f32(1, own, wide), *[shape_bf16(1, own, wide)] * (outer - 1)),
        "outer_terms", keep[None], *[recv[None] for recv in recvs],
    )
    keep, shifted = lax.optimization_barrier((keep, shifted))
    recvs = [
        permute(sends[k - 1], lambda i, n, k=k: i ^ (k * 2 * middle))
        for k in reversed(range(1, outer))
    ]
    input_grad = input_grad_call(shifted, masks, turned_taps)
    (summed,) = small_call(
        functools.partial(last_kernel, scale_factor),
        (shape_f32(1, own, wide),),
        "last_sum", keep, *recvs,
    )
    return layer_output, input_grad, summed[0]


def solution(mesh):
    return jax.shard_map(
        shards,
        mesh=mesh,
        in_specs=(
            P(("groups", "tiles"), None, None, None),
            P(("groups", "tiles"), None, None, None),
            P(),
            P("tiles", None),
            P("tiles", None, None),
        ),
        out_specs=(
            P(("groups", "tiles"), None, None, None),
            P(("groups", "tiles"), None, None, None),
            P(("groups", "tiles"), None),
        ),
        check_vma=False,
    )
```

```python
import functools
import math

import jax
import jax.numpy as jnp
from jax import lax
from jax.experimental import pallas as pl
from jax.experimental.pallas import tpu as pltpu
from jax.sharding import PartitionSpec as P

STEP = 2
BF16 = jnp.bfloat16
F32 = jnp.float32
GELU_SCALE = math.sqrt(2.0 / math.pi)
GELU_CUBIC = 0.044715
VMEM_BYTES = 16 << 20
LOAD_BYTES = 102 << 19

SMEM = pl.BlockSpec(memory_space=pltpu.SMEM)
VMEM = pl.BlockSpec(memory_space=pltpu.VMEM)
HBM = pl.BlockSpec(memory_space=pltpu.HBM)


def gelu_pair(h):
    h2 = h * h
    t = jnp.tanh(h * (GELU_SCALE + (GELU_SCALE * GELU_CUBIC) * h2))
    half_up = 0.5 + 0.5 * t
    activated = h * half_up
    derivative = half_up + h * (0.5 - 0.5 * t * t) * (
        GELU_SCALE + (3.0 * GELU_CUBIC * GELU_SCALE) * h2
    )
    return activated, derivative


def present_bf16(entry):
    return jnp.where(entry >= 0, 1.0, 0.0).astype(BF16)


def column_masks(mask):
    turned = mask.astype(F32).T
    side = turned.shape[0]
    return [
        jnp.broadcast_to(turned[:, r : r + 1], (side, 256)).astype(BF16)
        for r in range(turned.shape[1])
    ]


def edge_selector(rows, cols, picked):
    shape = (len(picked) * rows, rows * cols)
    out = lax.broadcasted_iota(jnp.int32, shape, 0)
    src = lax.broadcasted_iota(jnp.int32, shape, 1)
    want_row = out % rows
    want_col = picked[0] + out // rows
    return jnp.where(src == want_row * cols + want_col, 1.0, 0.0).astype(BF16)


def dot(a, b):
    return jnp.dot(a, b, preferred_element_type=F32)


def local_id(entry, slots):
    return jnp.where(entry < 0, -1, lax.rem(entry, slots))


def start_all(copies):
    for copy in copies:
        copy.start()
    return copies


def is_even():
    return lax.rem(lax.axis_index("tiles"), 2) == 0


def split_sides(west, east, across_ref, pair_ref):
    even = is_even()
    across_ref[...] = jnp.where(even, west, east).reshape(across_ref.shape)
    pair_ref[...] = jnp.where(even, east, west).reshape(pair_ref.shape)


def join_sides(across, pair):
    even = is_even()
    return jnp.where(even, across, pair), jnp.where(even, pair, across)


def load_kernel(x_hbm, cot_hbm, xe_ref, cote_ref, x_ref, cot_ref, sems):
    slots, rows, cols, ch = x_ref.shape
    half = cols // 2
    x_in, cot_in = (
        start_all(
            [
                pltpu.make_async_copy(src.at[s], dst.at[s], sems.at[i * slots + s])
                for s in range(slots)
            ]
        )
        for i, (src, dst) in enumerate(((x_hbm, x_ref), (cot_hbm, cot_ref)))
    )
    sel = [
        edge_selector(rows, half, list(range(0, 4))),
        edge_selector(rows, half, list(range(half - 4, half))),
    ]
    for s in range(slots):
        x_in[s].wait()
        for side in range(2):
            tiles = slice(side * half, side * half + half)
            x = dot(sel[side], x_ref[s, :, tiles].reshape(rows * half, ch)).astype(BF16)
            xe_ref[s, side * 4 : side * 4 + 4] = x.reshape(4, rows, ch)
    for s in range(slots):
        cot_in[s].wait()
        for side in range(2):
            tiles = slice(side * half, side * half + half)
            pick = sel[side][: 2 * rows] if side == 0 else sel[side][2 * rows :]
            c = dot(pick, cot_ref[s, :, tiles].reshape(rows * half, ch)).astype(BF16)
            cote_ref[side, s] = c.reshape(2, rows, ch)


def mask_kernel(raw_ref, raw_cot_ref, ms, across_ref, pair_ref, xe_ref, cote_ref):
    slots, _, rows, ch = raw_ref.shape
    cols = ms.shape[2]
    for s in range(slots):
        mask = ms[s].astype(F32)
        for side in range(2):
            for k in range(4):
                at = k if side == 0 else cols - 4 + k
                ocean = jnp.broadcast_to(mask[:, at : at + 1], (rows, ch)).astype(BF16)
                xe_ref[s, side * 4 + k] = raw_ref[s, side * 4 + k] * ocean
                outer = k if side == 0 else k - 2
                if 0 <= outer < 2:
                    cote_ref[side, s, outer] = raw_cot_ref[side, s, outer] * ocean
    split_sides(xe_ref[:, 0:2], xe_ref[:, 6:8], across_ref, pair_ref)


def interior_kernel(
    own, nbr_ref, x_ref, cot_ref, w_ref, ms,
    out_ref, grad_ref, dw_ref, xc, gt,
    mk,
):
    slots, rows, cols, ch = x_ref.shape
    zeros = jnp.zeros((rows, STEP, ch), BF16)
    for s in range(slots):
        for r, line in enumerate(column_masks(ms[s])):
            mk[s, r] = line
    for s in range(slots):
        xm = x_ref[s] * mk[s]
        xc[s, STEP : rows + STEP, :, ch : 2 * ch] = xm
        xc[s, STEP : rows + STEP, :, 0:ch] = jnp.concatenate(
            [zeros, xm[:, : cols - STEP]], axis=1
        )
        xc[s, STEP : rows + STEP, :, 2 * ch :] = jnp.concatenate([xm[:, STEP:], zeros], axis=1)
    for s in range(slots):
        north, south = local_id(nbr_ref[s, 0], slots), local_id(nbr_ref[s, 1], slots)
        xc[s, 0:STEP] = xc[jnp.maximum(north, 0), rows : rows + STEP] * present_bf16(north)
        xc[s, rows + STEP :] = xc[jnp.maximum(south, 0), STEP : 2 * STEP] * present_bf16(south)

    block = 8
    column = lax.broadcasted_iota(jnp.int32, (block, cols, ch), 1)
    inside = jnp.where((column >= STEP) & (column < cols - STEP), 1.0, 0.0).astype(BF16)
    for s in range(slots):
        for r0 in range(0, rows, block):
            acc = None
            for a in range(3):
                window = xc[s, r0 + STEP * a : r0 + STEP * a + block].reshape(block * cols, 3 * ch)
                term = dot(window, w_ref[a])
                acc = term if acc is None else acc + term
            activated, derivative = gelu_pair(acc)
            ocean = mk[s, r0 : r0 + block]
            xm = xc[s, r0 + STEP : r0 + STEP + block, :, ch : 2 * ch].reshape(block * cols, ch)
            out = (xm.astype(F32) + activated).astype(BF16).reshape(block, cols, ch)
            out_ref[s, r0 : r0 + block] = out * ocean
            cot = (cot_ref[s, r0 : r0 + block] * ocean) * inside
            g = (cot.reshape(block * cols, ch).astype(F32) * derivative).astype(BF16)
            grad_ref[s, r0 : r0 + block] = g.reshape(block, cols, ch)
            turn_rows(gt.at[s], g, r0 * cols, own)

    rank = dw_ref.shape[0]
    place = 0 if own is None else other_half(rank)
    for a in range(3):
        dw_ref[:, a * 3 * ch : (a + 1) * 3 * ch] = tap_terms(gt, xc, a, place, rank)


def half_of(core, rank):
    return pl.multiple_of(core * rank, rank)


def own_half(rank):
    return half_of(lax.rem(lax.axis_index("tiles"), 2), rank)


def other_half(rank):
    return half_of(1 - lax.rem(lax.axis_index("tiles"), 2), rank)


def tap_terms(gt, xc, a, place, rank):
    slots, _, cells = gt.shape
    rows = xc.shape[1] - 2 * STEP
    wide = xc.shape[3]
    grads = [gt[s, pl.ds(place, rank), :] for s in range(slots)]
    windows = [xc[s, STEP * a : STEP * a + rows].reshape(cells, wide) for s in range(slots)]
    return dot(jnp.concatenate(grads, axis=1), jnp.concatenate(windows, axis=0))


def turn_rows(gt, g, first, own):
    turned = g.T
    ch, cells = turned.shape
    if own is None:
        gt[:, first : first + cells] = turned
        return
    for j in range(ch // own):
        to = (j % 2) * (ch // 2) + (j // 2) * own
        gt[to : to + own, first : first + cells] = turned[j * own : (j + 1) * own]


def stack_rows(own, north, south, entry_n, entry_s):
    rows = own.shape[1]
    above = north[:, rows - STEP :] * present_bf16(entry_n)
    below = south[:, :STEP] * present_bf16(entry_s)
    return jnp.concatenate([above, own, below], axis=1)


def edge_kernel(
    own, nbr_ref, across_ref, pair_ref, xe_ref, cote_ref, w_ref, dwi_ref,
    gacross_ref, gpair_ref, ge_ref, oe_ref, dw_ref, win, gt,
    sides,
):
    slots, _, rows, ch = xe_ref.shape
    sides[0], sides[1] = join_sides(across_ref[...], pair_ref[...])

    def local(s, column):
        return local_id(nbr_ref[s, column], slots)

    for s in range(slots):
        for side in range(2):
            for b in range(3):
                halo = (side == 0 and b == 0) or (side == 1 and b == 2)
                if halo:
                    src = sides.at[side]
                    mid, top, low = (2, 4, 6) if side == 0 else (3, 5, 7)
                    e_mid, e_top, e_low = local(s, mid), local(s, top), local(s, low)
                    middle = src[jnp.maximum(e_mid, 0)] * present_bf16(e_mid)
                    north = src[jnp.maximum(e_top, 0)]
                    south = src[jnp.maximum(e_low, 0)]
                else:
                    at = 2 * (b - 1) if side == 0 else 4 + 2 * b
                    e_top, e_low = local(s, 0), local(s, 1)
                    middle = xe_ref[s, at : at + 2]
                    north = xe_ref[jnp.maximum(e_top, 0), at : at + 2]
                    south = xe_ref[jnp.maximum(e_low, 0), at : at + 2]
                tall = stack_rows(middle, north, south, e_top, e_low)
                for a in range(3):
                    win[a, side, s, :, :, b * ch : (b + 1) * ch] = tall[
                        :, STEP * a : STEP * a + rows
                    ]
    cells = 2 * slots * 2 * rows
    acc = None
    for a in range(3):
        term = dot(win[a].reshape(cells, 3 * ch), w_ref[a])
        acc = term if acc is None else acc + term
    activated, derivative = gelu_pair(acc)
    x_own = win[1, :, :, :, :, ch : 2 * ch].reshape(cells, ch)
    oe_ref[...] = (x_own.astype(F32) + activated).astype(BF16).reshape(oe_ref.shape)
    g = (cote_ref[...].reshape(cells, ch).astype(F32) * derivative).astype(BF16)
    ge_ref[...] = g.reshape(ge_ref.shape)
    split_sides(g[: cells // 2], g[cells // 2 :], gacross_ref, gpair_ref)
    turn_rows(gt, g, 0, own)
    rank = dw_ref.shape[0]
    place = 0 if own is None else other_half(rank)
    turned = gt[pl.ds(place, rank), :]
    for a in range(3):
        span = slice(a * 3 * ch, (a + 1) * 3 * ch)
        total = dwi_ref[:, span] + dot(turned, win[a].reshape(cells, 3 * ch))
        dw_ref[:, span] = total.astype(dw_ref.dtype)


def keep_kernel(xc, gt, win, edge_gt, keep_ref):
    rank = keep_ref.shape[0]
    wide = xc.shape[3]
    place = own_half(rank)
    turned = edge_gt[pl.ds(place, rank), :]
    for a in range(3):
        edge = dot(turned, win[a].reshape(edge_gt.shape[1], wide))
        keep_ref[:, a * wide : (a + 1) * wide] = tap_terms(gt, xc, a, place, rank) + edge


def spread_selector(rows, cols, first):
    shape = (rows * cols, 2 * rows)
    out = lax.broadcasted_iota(jnp.int32, shape, 0)
    src = lax.broadcasted_iota(jnp.int32, shape, 1)
    want = (out % cols - first) * rows + out // cols
    return jnp.where((src == want) & (out % cols >= first) & (out % cols < first + 2), 1.0, 0.0).astype(BF16)


def spread_edge(sel, edge):
    _, rows, ch = edge.shape
    return dot(sel, edge.reshape(2 * rows, ch)).astype(BF16).reshape(rows, -1, ch)


def gradient_kernel(
    nbr_ref, gi_ref, oi_ref, ge_ref, oe_ref, mask_ref, w_ref,
    out_hbm, gc, mk, wt_ref,
    out_ref, sems,
):
    slots, rows, cols, ch = gi_ref.shape
    half = cols // 2
    zeros = jnp.zeros((rows, STEP, ch), BF16)
    low = spread_selector(rows, half, 0)
    high = spread_selector(rows, half, half - 2)
    column = lax.broadcasted_iota(jnp.int32, (rows, half, ch), 1)
    stores = []
    for s in range(slots):
        for r, line in enumerate(column_masks(mask_ref[s])):
            mk[s, r] = line
        out_low = jnp.where(column < STEP, spread_edge(low, oe_ref[0, s]), oi_ref[s, :, :half])
        out_ref[s, :, :half] = out_low * mk[s, :, :half]
        out_high = jnp.where(
            column >= half - STEP, spread_edge(high, oe_ref[1, s]), oi_ref[s, :, half:]
        )
        out_ref[s, :, half:] = out_high * mk[s, :, half:]
        stores += start_all([pltpu.make_async_copy(out_ref.at[s], out_hbm.at[s], sems.at[s])])
    for s in range(slots):
        g = jnp.concatenate(
            [
                gi_ref[s, :, :half] + spread_edge(low, ge_ref[0, s]),
                gi_ref[s, :, half:] + spread_edge(high, ge_ref[1, s]),
            ],
            axis=1,
        )
        gc[s, STEP : rows + STEP, :, ch : 2 * ch] = g
        gc[s, STEP : rows + STEP, :, 2 * ch :] = jnp.concatenate(
            [zeros, g[:, : cols - STEP]], axis=1
        )
        gc[s, STEP : rows + STEP, :, 0:ch] = jnp.concatenate([g[:, STEP:], zeros], axis=1)
    for s in range(slots):
        north, south = local_id(nbr_ref[s, 0], slots), local_id(nbr_ref[s, 1], slots)
        gc[s, 0:STEP] = gc[jnp.maximum(north, 0), rows : rows + STEP] * present_bf16(north)
        gc[s, rows + STEP :] = gc[jnp.maximum(south, 0), STEP : 2 * STEP] * present_bf16(south)
    for a in range(3):
        for b in range(3):
            lanes = slice(b * ch, (b + 1) * ch)
            wt_ref[a, lanes] = w_ref[a, lanes].T
    for copy in stores:
        copy.wait()


def input_grad_kernel(
    nbr_ref, gc, mk, across_ref, pair_ref, cot_ref, wt_ref,
    ig_hbm,
    ig_ref, hs, ht, sems,
):
    slots, rows, cols, ch = cot_ref.shape
    half = cols // 2
    halos = join_sides(across_ref[...], pair_ref[...])
    for side in range(2):
        sel = spread_selector(rows, half, 0 if side == 0 else half - 2)
        for s in range(slots):
            hs[side, s] = spread_edge(sel, halos[side][s])
    for s in range(slots):
        for side, entries in enumerate(((4, 2, 6), (5, 3, 7))):
            lo, lanes = (0, 2 * ch) if side == 0 else (half, 0)
            for column, span, at in zip(
                entries,
                (slice(rows - STEP, rows), slice(0, rows), slice(0, STEP)),
                (slice(0, STEP), slice(STEP, rows + STEP), slice(rows + STEP, None)),
            ):
                entry = local_id(nbr_ref[s, column], slots)
                halo = hs[side, jnp.maximum(entry, 0), span] * present_bf16(entry)
                ht[side, s, at] = gc[s, at, lo : lo + half, lanes : lanes + ch] + halo
    block = 8
    stores = []
    for s in range(slots):
        for r0 in range(0, rows, block):
            acc = None
            for a in range(3):
                at = slice(r0 + STEP * (2 - a), r0 + STEP * (2 - a) + block)
                window = jnp.concatenate(
                    [
                        jnp.concatenate([gc[s, at, :half, :ch], ht[1, s, at]], axis=1),
                        gc[s, at, :, ch : 2 * ch],
                        jnp.concatenate([ht[0, s, at], gc[s, at, half:, 2 * ch :]], axis=1),
                    ],
                    axis=2,
                )
                term = dot(window.reshape(block * cols, 3 * ch), wt_ref[a])
                acc = term if acc is None else acc + term
            cot = cot_ref[s, r0 : r0 + block].reshape(block * cols, ch).astype(F32)
            ig = (cot + acc).astype(BF16).reshape(block, cols, ch)
            ig_ref[s, r0 : r0 + block] = ig * mk[s, r0 : r0 + block]
        stores += start_all([pltpu.make_async_copy(ig_ref.at[s], ig_hbm.at[s], sems.at[s])])
    for copy in stores:
        copy.wait()


def permute(value, pairs_of):
    count = lax.axis_size("tiles")
    return lax.ppermute(value, "tiles", [(i, pairs_of(i, count)) for i in range(count)])


def swap_halos(across, pair):
    across = permute(across, lambda i, n: (i - 1 if i % 2 == 0 else i + 1) % n)
    return across, permute(pair, lambda i, n: i ^ 1)


def stage_sizes(count):
    rest = count // 2
    middle = 1
    while middle * middle * 4 <= rest:
        middle *= 2
    return rest // middle, middle, 2


def exchange_sum(total, axis, position, size, stride):
    acc = lax.dynamic_index_in_dim(total, position, axis, False)
    parts = []
    for k in range(1, size):
        other = lax.dynamic_index_in_dim(total, position ^ k, axis, False).astype(BF16)
        parts.append(permute(other, lambda i, n: i ^ (k * stride)))
    for part in parts:
        acc = acc + part.astype(F32)
    return acc


def scatter_sum(dw, device):
    count = lax.axis_size("tiles")
    outer, middle, core = stage_sizes(count)
    own_rows = dw.shape[0] // count
    total = dw.reshape(outer, middle, core, own_rows, dw.shape[1])
    c, y, z = device % core, device // core % middle, device // (core * middle)
    total = exchange_sum(total, 2, c, core, 1)
    total = exchange_sum(total, 1, y, middle, core)
    return exchange_sum(total, 0, z, outer, core * middle)


def split_kernel(stride, keep_ref, *refs):
    size = keep_ref.shape[1]
    count = len(refs) - size
    recvs, keep_out, sends = refs[:count], refs[count], refs[count + 1 :]
    place = lax.rem(lax.axis_index("tiles") // stride, size)
    for i in range(keep_ref.shape[0]):
        for k in range(size):
            acc = keep_ref[i, place ^ k]
            for recv in recvs:
                acc = acc + recv[i, place ^ k].astype(F32)
            if k == 0:
                keep_out[i] = acc
            else:
                sends[k - 1][i] = acc.astype(BF16)


def last_kernel(scale, keep_ref, *refs):
    *recvs, out_ref = refs
    acc = keep_ref[...]
    for recv in recvs:
        acc = acc + recv[...].astype(F32)
    out_ref[...] = acc * scale


def small_call(kernel, out_shapes, name, *args):
    return pl.pallas_call(
        kernel,
        out_shape=out_shapes,
        in_specs=[VMEM] * len(args),
        out_specs=tuple(VMEM for _ in out_shapes),
        compiler_params=pltpu.CompilerParams(vmem_limit_bytes=8 << 20),
        name=name,
    )(*args)


def shape_f32(*dims):
    return jax.ShapeDtypeStruct(dims, F32)


def shape_bf16(*dims):
    return jax.ShapeDtypeStruct(dims, BF16)


def shards(input_field, cotangent, weight, neighbours, land_mask):
    device = lax.axis_index("tiles")
    count = lax.axis_size("tiles")
    slots, rows, cols, ch = input_field.shape
    taps = weight.reshape(3, 3 * ch, ch)
    params = pltpu.CompilerParams(vmem_limit_bytes=VMEM_BYTES)
    side_columns = (slots, STEP, rows, ch)
    field = input_field.shape
    own = ch // count if ch // count % 16 == 0 else None
    outer, middle, _ = stage_sizes(count)

    raw_edge, raw_cot, field_in, cot_in = pl.pallas_call(
        load_kernel,
        out_shape=(
            shape_bf16(slots, 8, rows, ch),
            shape_bf16(2, *side_columns),
            shape_bf16(*field),
            shape_bf16(*field),
        ),
        in_specs=[HBM] * 2,
        out_specs=(VMEM,) * 4,
        scratch_shapes=[pltpu.SemaphoreType.DMA((2 * slots,))],
        compiler_params=pltpu.CompilerParams(vmem_limit_bytes=LOAD_BYTES),
        name="load",
    )(input_field, cotangent)
    across, pair, x_edge, cot_edge = small_call(
        mask_kernel,
        (
            shape_bf16(*side_columns),
            shape_bf16(*side_columns),
            shape_bf16(slots, 8, rows, ch),
            shape_bf16(2, *side_columns),
        ),
        "mask_edges", raw_edge, raw_cot, land_mask,
    )
    across, pair = swap_halos(across, pair)

    rank = ch if own is None else ch // 2
    out_inner, grad_inner, dw_inner, windows, turned = pl.pallas_call(
        functools.partial(interior_kernel, own),
        out_shape=(
            shape_bf16(*field),
            shape_bf16(*field),
            shape_f32(rank, 9 * ch),
            shape_bf16(slots, rows + 2 * STEP, cols, 3 * ch),
            shape_bf16(slots, ch, rows * cols),
        ),
        in_specs=[SMEM] + [VMEM] * 4,
        out_specs=(VMEM,) * 5,
        scratch_shapes=[pltpu.VMEM(field, BF16)],
        compiler_params=params,
        cost_estimate=pl.CostEstimate(
            flops=4 * 9 * slots * rows * cols * ch * ch, bytes_accessed=8 << 20, transcendentals=0
        ),
        name="interior",
    )(neighbours, field_in, cot_in, taps, land_mask)

    grad_across, grad_pair, grad_edge, out_edge, dw, edge_windows, edge_turned = pl.pallas_call(
        functools.partial(edge_kernel, own),
        out_shape=(
            shape_bf16(*side_columns),
            shape_bf16(*side_columns),
            shape_bf16(2, *side_columns),
            shape_bf16(2, *side_columns),
            shape_f32(ch, 9 * ch) if own is None else shape_bf16(rank, 9 * ch),
            shape_bf16(3, 2, slots, STEP, rows, 3 * ch),
            shape_bf16(ch, 4 * slots * rows),
        ),
        in_specs=[SMEM] + [VMEM] * 6,
        out_specs=(VMEM,) * 7,
        scratch_shapes=[pltpu.VMEM((2, *side_columns), BF16)],
        compiler_params=params,
        cost_estimate=pl.CostEstimate(
            flops=4 * 9 * slots * rows * 4 * ch * ch, bytes_accessed=6 << 20, transcendentals=0
        ),
        name="edges",
    )(neighbours, across, pair, x_edge, cot_edge, taps, dw_inner)

    grad_across, grad_pair = swap_halos(grad_across, grad_pair)

    def gradient_call(grad_edge):
        return pl.pallas_call(
            gradient_kernel,
            out_shape=(
                shape_bf16(*field),
                shape_bf16(slots, rows + 2 * STEP, cols, 3 * ch),
                shape_bf16(*field),
                shape_bf16(3, 3 * ch, ch),
            ),
            in_specs=[SMEM] + [VMEM] * 6,
            out_specs=(HBM, VMEM, VMEM, VMEM),
            scratch_shapes=[pltpu.VMEM(field, BF16), pltpu.SemaphoreType.DMA((slots,))],
            compiler_params=params,
            cost_estimate=pl.CostEstimate(flops=1 << 31, bytes_accessed=0, transcendentals=0),
            name="gradient",
        )(neighbours, grad_inner, out_inner, grad_edge, out_edge, land_mask, taps)

    def input_grad_call(shifted, masks, turned_taps):
        return pl.pallas_call(
            input_grad_kernel,
            out_shape=shape_bf16(*field),
            in_specs=[SMEM] + [VMEM] * 6,
            out_specs=HBM,
            scratch_shapes=[
                pltpu.VMEM(field, BF16),
                pltpu.VMEM((2, slots, rows, cols // 2, ch), BF16),
                pltpu.VMEM((2, slots, rows + 2 * STEP, cols // 2, ch), BF16),
                pltpu.SemaphoreType.DMA((slots,)),
            ],
            compiler_params=params,
            cost_estimate=pl.CostEstimate(
                flops=2 * 9 * slots * rows * cols * ch * ch,
                bytes_accessed=8 << 20,
                transcendentals=0,
            ),
            name="input_grad",
        )(neighbours, shifted, masks, grad_across, grad_pair, cot_in, turned_taps)

    scale_factor = 1.0 / (rows * math.sqrt(slots * count))
    if own is None:
        summed = scatter_sum(dw, device)
        layer_output, shifted, masks, turned_taps = gradient_call(grad_edge)
        return layer_output, input_grad_call(shifted, masks, turned_taps), summed * scale_factor

    wide = 9 * ch
    recv = permute(dw, lambda i, n: i ^ 1)
    (keep,) = pl.pallas_call(
        keep_kernel,
        out_shape=(shape_f32(rank, wide),),
        in_specs=[VMEM] * 4,
        out_specs=(VMEM,),
        compiler_params=params,
        cost_estimate=pl.CostEstimate(
            flops=9 * slots * rows * (cols + 4) * ch * ch, bytes_accessed=0, transcendentals=0
        ),
        name="keep",
    )(windows, turned, edge_windows, edge_turned)
    whole = (outer, middle, own, wide)
    keep, *sends = small_call(
        functools.partial(split_kernel, 2),
        (shape_f32(outer, own, wide), *[shape_bf16(outer, own, wide)] * (middle - 1)),
        "middle_terms", keep.reshape(whole), recv.reshape(whole),
    )
    recvs = [permute(sends[k - 1], lambda i, n, k=k: i ^ (k * 2)) for k in range(1, middle)]
    keep, grad_edge = lax.optimization_barrier((keep, grad_edge))
    layer_output, shifted, masks, turned_taps = gradient_call(grad_edge)
    keep, *recvs, shifted = lax.optimization_barrier((keep, *recvs, shifted))
    keep, *sends = small_call(
        functools.partial(split_kernel, 2 * middle),
        (shape_f32(1, own, wide), *[shape_bf16(1, own, wide)] * (outer - 1)),
        "outer_terms", keep[None], *[recv[None] for recv in recvs],
    )
    keep, shifted = lax.optimization_barrier((keep, shifted))
    recvs = [
        permute(sends[k - 1], lambda i, n, k=k: i ^ (k * 2 * middle))
        for k in reversed(range(1, outer))
    ]
    input_grad = input_grad_call(shifted, masks, turned_taps)
    (summed,) = small_call(
        functools.partial(last_kernel, scale_factor),
        (shape_f32(1, own, wide),),
        "last_sum", keep, *recvs,
    )
    return layer_output, input_grad, summed[0]


def solution(mesh):
    return jax.shard_map(
        shards,
        mesh=mesh,
        in_specs=(
            P(("groups", "tiles"), None, None, None),
            P(("groups", "tiles"), None, None, None),
            P(),
            P("tiles", None),
            P("tiles", None, None),
        ),
        out_specs=(
            P(("groups", "tiles"), None, None, None),
            P(("groups", "tiles"), None, None, None),
            P(("groups", "tiles"), None),
        ),
        check_vma=False,
    )
```

```python
import functools
import math

import jax
import jax.numpy as jnp
from jax import lax
from jax.experimental import pallas as pl
from jax.experimental.pallas import tpu as pltpu
from jax.sharding import PartitionSpec as P

STEP = 2
BF16 = jnp.bfloat16
F32 = jnp.float32
GELU_SCALE = math.sqrt(2.0 / math.pi)
GELU_CUBIC = 0.044715
VMEM_BYTES = 16 << 20
LOAD_BYTES = 102 << 19

SMEM = pl.BlockSpec(memory_space=pltpu.SMEM)
VMEM = pl.BlockSpec(memory_space=pltpu.VMEM)
HBM = pl.BlockSpec(memory_space=pltpu.HBM)


def gelu_pair(h):
    h2 = h * h
    t = jnp.tanh(h * (GELU_SCALE + (GELU_SCALE * GELU_CUBIC) * h2))
    half_up = 0.5 + 0.5 * t
    activated = h * half_up
    derivative = half_up + h * (0.5 - 0.5 * t * t) * (
        GELU_SCALE + (3.0 * GELU_CUBIC * GELU_SCALE) * h2
    )
    return activated, derivative


def present_bf16(entry):
    return jnp.where(entry >= 0, 1.0, 0.0).astype(BF16)


def column_masks(mask):
    turned = mask.astype(F32).T
    side = turned.shape[0]
    return [
        jnp.broadcast_to(turned[:, r : r + 1], (side, 256)).astype(BF16)
        for r in range(turned.shape[1])
    ]


def edge_selector(rows, cols, picked):
    shape = (len(picked) * rows, rows * cols)
    out = lax.broadcasted_iota(jnp.int32, shape, 0)
    src = lax.broadcasted_iota(jnp.int32, shape, 1)
    want_row = out % rows
    want_col = picked[0] + out // rows
    return jnp.where(src == want_row * cols + want_col, 1.0, 0.0).astype(BF16)


def dot(a, b):
    return jnp.dot(a, b, preferred_element_type=F32)


def local_id(entry, slots):
    return jnp.where(entry < 0, -1, lax.rem(entry, slots))


def start_all(copies):
    for copy in copies:
        copy.start()
    return copies


def is_even():
    return lax.rem(lax.axis_index("tiles"), 2) == 0


def split_sides(west, east, across_ref, pair_ref):
    even = is_even()
    across_ref[...] = jnp.where(even, west, east).reshape(across_ref.shape)
    pair_ref[...] = jnp.where(even, east, west).reshape(pair_ref.shape)


def join_sides(across, pair):
    even = is_even()
    return jnp.where(even, across, pair), jnp.where(even, pair, across)


def load_kernel(x_hbm, cot_hbm, xe_ref, cote_ref, x_ref, cot_ref, sems):
    slots, rows, cols, ch = x_ref.shape
    half = cols // 2
    x_in, cot_in = (
        start_all(
            [
                pltpu.make_async_copy(src.at[s], dst.at[s], sems.at[i * slots + s])
                for s in range(slots)
            ]
        )
        for i, (src, dst) in enumerate(((x_hbm, x_ref), (cot_hbm, cot_ref)))
    )
    sel = [
        edge_selector(rows, half, list(range(0, 4))),
        edge_selector(rows, half, list(range(half - 4, half))),
    ]
    for s in range(slots):
        x_in[s].wait()
        for side in range(2):
            tiles = slice(side * half, side * half + half)
            x = dot(sel[side], x_ref[s, :, tiles].reshape(rows * half, ch)).astype(BF16)
            xe_ref[s, side * 4 : side * 4 + 4] = x.reshape(4, rows, ch)
    for s in range(slots):
        cot_in[s].wait()
        for side in range(2):
            tiles = slice(side * half, side * half + half)
            pick = sel[side][: 2 * rows] if side == 0 else sel[side][2 * rows :]
            c = dot(pick, cot_ref[s, :, tiles].reshape(rows * half, ch)).astype(BF16)
            cote_ref[side, s] = c.reshape(2, rows, ch)


def mask_kernel(raw_ref, raw_cot_ref, ms, across_ref, pair_ref, xe_ref, cote_ref):
    slots, _, rows, ch = raw_ref.shape
    cols = ms.shape[2]
    for s in range(slots):
        mask = ms[s].astype(F32)
        for side in range(2):
            for k in range(4):
                at = k if side == 0 else cols - 4 + k
                ocean = jnp.broadcast_to(mask[:, at : at + 1], (rows, ch)).astype(BF16)
                xe_ref[s, side * 4 + k] = raw_ref[s, side * 4 + k] * ocean
                outer = k if side == 0 else k - 2
                if 0 <= outer < 2:
                    cote_ref[side, s, outer] = raw_cot_ref[side, s, outer] * ocean
    split_sides(xe_ref[:, 0:2], xe_ref[:, 6:8], across_ref, pair_ref)


def interior_kernel(
    own, nbr_ref, x_ref, cot_ref, w_ref, ms,
    out_ref, grad_ref, dw_ref, xc, gt,
    mk,
):
    slots, rows, cols, ch = x_ref.shape
    zeros = jnp.zeros((rows, STEP, ch), BF16)
    for s in range(slots):
        for r, line in enumerate(column_masks(ms[s])):
            mk[s, r] = line
    for s in range(slots):
        xm = x_ref[s] * mk[s]
        xc[s, STEP : rows + STEP, :, ch : 2 * ch] = xm
        xc[s, STEP : rows + STEP, :, 0:ch] = jnp.concatenate(
            [zeros, xm[:, : cols - STEP]], axis=1
        )
        xc[s, STEP : rows + STEP, :, 2 * ch :] = jnp.concatenate([xm[:, STEP:], zeros], axis=1)
    for s in range(slots):
        north, south = local_id(nbr_ref[s, 0], slots), local_id(nbr_ref[s, 1], slots)
        xc[s, 0:STEP] = xc[jnp.maximum(north, 0), rows : rows + STEP] * present_bf16(north)
        xc[s, rows + STEP :] = xc[jnp.maximum(south, 0), STEP : 2 * STEP] * present_bf16(south)

    block = 8
    column = lax.broadcasted_iota(jnp.int32, (block, cols, ch), 1)
    inside = jnp.where((column >= STEP) & (column < cols - STEP), 1.0, 0.0).astype(BF16)
    for s in range(slots):
        for r0 in range(0, rows, block):
            acc = None
            for a in range(3):
                window = xc[s, r0 + STEP * a : r0 + STEP * a + block].reshape(block * cols, 3 * ch)
                term = dot(window, w_ref[a])
                acc = term if acc is None else acc + term
            activated, derivative = gelu_pair(acc)
            ocean = mk[s, r0 : r0 + block]
            xm = xc[s, r0 + STEP : r0 + STEP + block, :, ch : 2 * ch].reshape(block * cols, ch)
            out = (xm.astype(F32) + activated).astype(BF16).reshape(block, cols, ch)
            out_ref[s, r0 : r0 + block] = out * ocean
            cot = (cot_ref[s, r0 : r0 + block] * ocean) * inside
            g = (cot.reshape(block * cols, ch).astype(F32) * derivative).astype(BF16)
            grad_ref[s, r0 : r0 + block] = g.reshape(block, cols, ch)
            turn_rows(gt.at[s], g, r0 * cols, own)

    rank = dw_ref.shape[0]
    place = 0 if own is None else other_half(rank)
    for a in range(3):
        dw_ref[:, a * 3 * ch : (a + 1) * 3 * ch] = tap_terms(gt, xc, a, place, rank)


def half_of(core, rank):
    return pl.multiple_of(core * rank, rank)


def own_half(rank):
    return half_of(lax.rem(lax.axis_index("tiles"), 2), rank)


def other_half(rank):
    return half_of(1 - lax.rem(lax.axis_index("tiles"), 2), rank)


def tap_terms(gt, xc, a, place, rank):
    slots, _, cells = gt.shape
    rows = xc.shape[1] - 2 * STEP
    wide = xc.shape[3]
    grads = [gt[s, pl.ds(place, rank), :] for s in range(slots)]
    windows = [xc[s, STEP * a : STEP * a + rows].reshape(cells, wide) for s in range(slots)]
    return dot(jnp.concatenate(grads, axis=1), jnp.concatenate(windows, axis=0))


def turn_rows(gt, g, first, own):
    turned = g.T
    ch, cells = turned.shape
    if own is None:
        gt[:, first : first + cells] = turned
        return
    for j in range(ch // own):
        to = (j % 2) * (ch // 2) + (j // 2) * own
        gt[to : to + own, first : first + cells] = turned[j * own : (j + 1) * own]


def stack_rows(own, north, south, entry_n, entry_s):
    rows = own.shape[1]
    above = north[:, rows - STEP :] * present_bf16(entry_n)
    below = south[:, :STEP] * present_bf16(entry_s)
    return jnp.concatenate([above, own, below], axis=1)


def edge_kernel(
    own, nbr_ref, across_ref, pair_ref, xe_ref, cote_ref, w_ref, dwi_ref,
    gacross_ref, gpair_ref, ge_ref, oe_ref, dw_ref, win, gt,
    sides,
):
    slots, _, rows, ch = xe_ref.shape
    sides[0], sides[1] = join_sides(across_ref[...], pair_ref[...])

    def local(s, column):
        return local_id(nbr_ref[s, column], slots)

    for s in range(slots):
        for side in range(2):
            for b in range(3):
                halo = (side == 0 and b == 0) or (side == 1 and b == 2)
                if halo:
                    src = sides.at[side]
                    mid, top, low = (2, 4, 6) if side == 0 else (3, 5, 7)
                    e_mid, e_top, e_low = local(s, mid), local(s, top), local(s, low)
                    middle = src[jnp.maximum(e_mid, 0)] * present_bf16(e_mid)
                    north = src[jnp.maximum(e_top, 0)]
                    south = src[jnp.maximum(e_low, 0)]
                else:
                    at = 2 * (b - 1) if side == 0 else 4 + 2 * b
                    e_top, e_low = local(s, 0), local(s, 1)
                    middle = xe_ref[s, at : at + 2]
                    north = xe_ref[jnp.maximum(e_top, 0), at : at + 2]
                    south = xe_ref[jnp.maximum(e_low, 0), at : at + 2]
                tall = stack_rows(middle, north, south, e_top, e_low)
                for a in range(3):
                    win[a, side, s, :, :, b * ch : (b + 1) * ch] = tall[
                        :, STEP * a : STEP * a + rows
                    ]
    cells = 2 * slots * 2 * rows
    acc = None
    for a in range(3):
        term = dot(win[a].reshape(cells, 3 * ch), w_ref[a])
        acc = term if acc is None else acc + term
    activated, derivative = gelu_pair(acc)
    x_own = win[1, :, :, :, :, ch : 2 * ch].reshape(cells, ch)
    oe_ref[...] = (x_own.astype(F32) + activated).astype(BF16).reshape(oe_ref.shape)
    g = (cote_ref[...].reshape(cells, ch).astype(F32) * derivative).astype(BF16)
    ge_ref[...] = g.reshape(ge_ref.shape)
    split_sides(g[: cells // 2], g[cells // 2 :], gacross_ref, gpair_ref)
    turn_rows(gt, g, 0, own)
    rank = dw_ref.shape[0]
    place = 0 if own is None else other_half(rank)
    turned = gt[pl.ds(place, rank), :]
    for a in range(3):
        span = slice(a * 3 * ch, (a + 1) * 3 * ch)
        total = dwi_ref[:, span] + dot(turned, win[a].reshape(cells, 3 * ch))
        dw_ref[:, span] = total.astype(dw_ref.dtype)


def keep_kernel(xc, gt, win, edge_gt, keep_ref):
    rank = keep_ref.shape[0]
    wide = xc.shape[3]
    place = own_half(rank)
    turned = edge_gt[pl.ds(place, rank), :]
    for a in range(3):
        edge = dot(turned, win[a].reshape(edge_gt.shape[1], wide))
        keep_ref[:, a * wide : (a + 1) * wide] = tap_terms(gt, xc, a, place, rank) + edge


def spread_selector(rows, cols, first):
    shape = (rows * cols, 2 * rows)
    out = lax.broadcasted_iota(jnp.int32, shape, 0)
    src = lax.broadcasted_iota(jnp.int32, shape, 1)
    want = (out % cols - first) * rows + out // cols
    return jnp.where((src == want) & (out % cols >= first) & (out % cols < first + 2), 1.0, 0.0).astype(BF16)


def spread_edge(sel, edge):
    _, rows, ch = edge.shape
    return dot(sel, edge.reshape(2 * rows, ch)).astype(BF16).reshape(rows, -1, ch)


def gradient_kernel(
    nbr_ref, gi_ref, oi_ref, ge_ref, oe_ref, mask_ref, w_ref,
    out_hbm, gc, mk, wt_ref,
    out_ref, sems,
):
    slots, rows, cols, ch = gi_ref.shape
    half = cols // 2
    zeros = jnp.zeros((rows, STEP, ch), BF16)
    low = spread_selector(rows, half, 0)
    high = spread_selector(rows, half, half - 2)
    column = lax.broadcasted_iota(jnp.int32, (rows, half, ch), 1)
    stores = []
    for s in range(slots):
        for r, line in enumerate(column_masks(mask_ref[s])):
            mk[s, r] = line
        out_low = jnp.where(column < STEP, spread_edge(low, oe_ref[0, s]), oi_ref[s, :, :half])
        out_ref[s, :, :half] = out_low * mk[s, :, :half]
        out_high = jnp.where(
            column >= half - STEP, spread_edge(high, oe_ref[1, s]), oi_ref[s, :, half:]
        )
        out_ref[s, :, half:] = out_high * mk[s, :, half:]
        stores += start_all([pltpu.make_async_copy(out_ref.at[s], out_hbm.at[s], sems.at[s])])
    for s in range(slots):
        g = jnp.concatenate(
            [
                gi_ref[s, :, :half] + spread_edge(low, ge_ref[0, s]),
                gi_ref[s, :, half:] + spread_edge(high, ge_ref[1, s]),
            ],
            axis=1,
        )
        gc[s, STEP : rows + STEP, :, ch : 2 * ch] = g
        gc[s, STEP : rows + STEP, :, 2 * ch :] = jnp.concatenate(
            [zeros, g[:, : cols - STEP]], axis=1
        )
        gc[s, STEP : rows + STEP, :, 0:ch] = jnp.concatenate([g[:, STEP:], zeros], axis=1)
    for s in range(slots):
        north, south = local_id(nbr_ref[s, 0], slots), local_id(nbr_ref[s, 1], slots)
        gc[s, 0:STEP] = gc[jnp.maximum(north, 0), rows : rows + STEP] * present_bf16(north)
        gc[s, rows + STEP :] = gc[jnp.maximum(south, 0), STEP : 2 * STEP] * present_bf16(south)
    for a in range(3):
        for b in range(3):
            lanes = slice(b * ch, (b + 1) * ch)
            wt_ref[a, lanes] = w_ref[a, lanes].T
    for copy in stores:
        copy.wait()


def input_grad_kernel(
    nbr_ref, gc, mk, across_ref, pair_ref, cot_ref, wt_ref,
    ig_hbm,
    ig_ref, hs, ht, sems,
):
    slots, rows, cols, ch = cot_ref.shape
    half = cols // 2
    halos = join_sides(across_ref[...], pair_ref[...])
    for side in range(2):
        sel = spread_selector(rows, half, 0 if side == 0 else half - 2)
        for s in range(slots):
            hs[side, s] = spread_edge(sel, halos[side][s])
    for s in range(slots):
        for side, entries in enumerate(((4, 2, 6), (5, 3, 7))):
            lo, lanes = (0, 2 * ch) if side == 0 else (half, 0)
            for column, span, at in zip(
                entries,
                (slice(rows - STEP, rows), slice(0, rows), slice(0, STEP)),
                (slice(0, STEP), slice(STEP, rows + STEP), slice(rows + STEP, None)),
            ):
                entry = local_id(nbr_ref[s, column], slots)
                halo = hs[side, jnp.maximum(entry, 0), span] * present_bf16(entry)
                ht[side, s, at] = gc[s, at, lo : lo + half, lanes : lanes + ch] + halo
    block = 8
    stores = []
    for s in range(slots):
        for r0 in range(0, rows, block):
            acc = None
            for a in range(3):
                at = slice(r0 + STEP * (2 - a), r0 + STEP * (2 - a) + block)
                window = jnp.concatenate(
                    [
                        jnp.concatenate([gc[s, at, :half, :ch], ht[1, s, at]], axis=1),
                        gc[s, at, :, ch : 2 * ch],
                        jnp.concatenate([ht[0, s, at], gc[s, at, half:, 2 * ch :]], axis=1),
                    ],
                    axis=2,
                )
                term = dot(window.reshape(block * cols, 3 * ch), wt_ref[a])
                acc = term if acc is None else acc + term
            cot = cot_ref[s, r0 : r0 + block].reshape(block * cols, ch).astype(F32)
            ig = (cot + acc).astype(BF16).reshape(block, cols, ch)
            ig_ref[s, r0 : r0 + block] = ig * mk[s, r0 : r0 + block]
            done = pl.ds(r0, block)
            stores += start_all(
                [
                    pltpu.make_async_copy(
                        ig_ref.at[s, done], ig_hbm.at[s, done], sems.at[s, r0 // block]
                    )
                ]
            )
    for copy in stores:
        copy.wait()


def permute(value, pairs_of):
    count = lax.axis_size("tiles")
    return lax.ppermute(value, "tiles", [(i, pairs_of(i, count)) for i in range(count)])


def swap_halos(across, pair):
    across = permute(across, lambda i, n: (i - 1 if i % 2 == 0 else i + 1) % n)
    return across, permute(pair, lambda i, n: i ^ 1)


def stage_sizes(count):
    rest = count // 2
    middle = 1
    while middle * middle * 4 <= rest:
        middle *= 2
    return rest // middle, middle, 2


def exchange_sum(total, axis, position, size, stride):
    acc = lax.dynamic_index_in_dim(total, position, axis, False)
    parts = []
    for k in range(1, size):
        other = lax.dynamic_index_in_dim(total, position ^ k, axis, False).astype(BF16)
        parts.append(permute(other, lambda i, n: i ^ (k * stride)))
    for part in parts:
        acc = acc + part.astype(F32)
    return acc


def scatter_sum(dw, device):
    count = lax.axis_size("tiles")
    outer, middle, core = stage_sizes(count)
    own_rows = dw.shape[0] // count
    total = dw.reshape(outer, middle, core, own_rows, dw.shape[1])
    c, y, z = device % core, device // core % middle, device // (core * middle)
    total = exchange_sum(total, 2, c, core, 1)
    total = exchange_sum(total, 1, y, middle, core)
    return exchange_sum(total, 0, z, outer, core * middle)


def split_kernel(stride, keep_ref, *refs):
    size = keep_ref.shape[1]
    count = len(refs) - size
    recvs, keep_out, sends = refs[:count], refs[count], refs[count + 1 :]
    place = lax.rem(lax.axis_index("tiles") // stride, size)
    for i in range(keep_ref.shape[0]):
        for k in range(size):
            acc = keep_ref[i, place ^ k]
            for recv in recvs:
                acc = acc + recv[i, place ^ k].astype(F32)
            if k == 0:
                keep_out[i] = acc
            else:
                sends[k - 1][i] = acc.astype(BF16)


def last_kernel(scale, keep_ref, *refs):
    *recvs, out_ref = refs
    acc = keep_ref[...]
    for recv in recvs:
        acc = acc + recv[...].astype(F32)
    out_ref[...] = acc * scale


def small_call(kernel, out_shapes, name, *args):
    return pl.pallas_call(
        kernel,
        out_shape=out_shapes,
        in_specs=[VMEM] * len(args),
        out_specs=tuple(VMEM for _ in out_shapes),
        compiler_params=pltpu.CompilerParams(vmem_limit_bytes=8 << 20),
        name=name,
    )(*args)


def shape_f32(*dims):
    return jax.ShapeDtypeStruct(dims, F32)


def shape_bf16(*dims):
    return jax.ShapeDtypeStruct(dims, BF16)


def shards(input_field, cotangent, weight, neighbours, land_mask):
    device = lax.axis_index("tiles")
    count = lax.axis_size("tiles")
    slots, rows, cols, ch = input_field.shape
    taps = weight.reshape(3, 3 * ch, ch)
    params = pltpu.CompilerParams(vmem_limit_bytes=VMEM_BYTES)
    side_columns = (slots, STEP, rows, ch)
    field = input_field.shape
    own = ch // count if ch // count % 16 == 0 else None
    outer, middle, _ = stage_sizes(count)

    raw_edge, raw_cot, field_in, cot_in = pl.pallas_call(
        load_kernel,
        out_shape=(
            shape_bf16(slots, 8, rows, ch),
            shape_bf16(2, *side_columns),
            shape_bf16(*field),
            shape_bf16(*field),
        ),
        in_specs=[HBM] * 2,
        out_specs=(VMEM,) * 4,
        scratch_shapes=[pltpu.SemaphoreType.DMA((2 * slots,))],
        compiler_params=pltpu.CompilerParams(vmem_limit_bytes=LOAD_BYTES),
        name="load",
    )(input_field, cotangent)
    across, pair, x_edge, cot_edge = small_call(
        mask_kernel,
        (
            shape_bf16(*side_columns),
            shape_bf16(*side_columns),
            shape_bf16(slots, 8, rows, ch),
            shape_bf16(2, *side_columns),
        ),
        "mask_edges", raw_edge, raw_cot, land_mask,
    )
    across, pair = swap_halos(across, pair)

    rank = ch if own is None else ch // 2
    out_inner, grad_inner, dw_inner, windows, turned = pl.pallas_call(
        functools.partial(interior_kernel, own),
        out_shape=(
            shape_bf16(*field),
            shape_bf16(*field),
            shape_f32(rank, 9 * ch),
            shape_bf16(slots, rows + 2 * STEP, cols, 3 * ch),
            shape_bf16(slots, ch, rows * cols),
        ),
        in_specs=[SMEM] + [VMEM] * 4,
        out_specs=(VMEM,) * 5,
        scratch_shapes=[pltpu.VMEM(field, BF16)],
        compiler_params=params,
        cost_estimate=pl.CostEstimate(
            flops=4 * 9 * slots * rows * cols * ch * ch, bytes_accessed=8 << 20, transcendentals=0
        ),
        name="interior",
    )(neighbours, field_in, cot_in, taps, land_mask)

    grad_across, grad_pair, grad_edge, out_edge, dw, edge_windows, edge_turned = pl.pallas_call(
        functools.partial(edge_kernel, own),
        out_shape=(
            shape_bf16(*side_columns),
            shape_bf16(*side_columns),
            shape_bf16(2, *side_columns),
            shape_bf16(2, *side_columns),
            shape_f32(ch, 9 * ch) if own is None else shape_bf16(rank, 9 * ch),
            shape_bf16(3, 2, slots, STEP, rows, 3 * ch),
            shape_bf16(ch, 4 * slots * rows),
        ),
        in_specs=[SMEM] + [VMEM] * 6,
        out_specs=(VMEM,) * 7,
        scratch_shapes=[pltpu.VMEM((2, *side_columns), BF16)],
        compiler_params=params,
        cost_estimate=pl.CostEstimate(
            flops=4 * 9 * slots * rows * 4 * ch * ch, bytes_accessed=6 << 20, transcendentals=0
        ),
        name="edges",
    )(neighbours, across, pair, x_edge, cot_edge, taps, dw_inner)

    grad_across, grad_pair = swap_halos(grad_across, grad_pair)

    def gradient_call(grad_edge):
        return pl.pallas_call(
            gradient_kernel,
            out_shape=(
                shape_bf16(*field),
                shape_bf16(slots, rows + 2 * STEP, cols, 3 * ch),
                shape_bf16(*field),
                shape_bf16(3, 3 * ch, ch),
            ),
            in_specs=[SMEM] + [VMEM] * 6,
            out_specs=(HBM, VMEM, VMEM, VMEM),
            scratch_shapes=[pltpu.VMEM(field, BF16), pltpu.SemaphoreType.DMA((slots,))],
            compiler_params=params,
            cost_estimate=pl.CostEstimate(flops=1 << 31, bytes_accessed=0, transcendentals=0),
            name="gradient",
        )(neighbours, grad_inner, out_inner, grad_edge, out_edge, land_mask, taps)

    def input_grad_call(shifted, masks, turned_taps):
        return pl.pallas_call(
            input_grad_kernel,
            out_shape=shape_bf16(*field),
            in_specs=[SMEM] + [VMEM] * 6,
            out_specs=HBM,
            scratch_shapes=[
                pltpu.VMEM(field, BF16),
                pltpu.VMEM((2, slots, rows, cols // 2, ch), BF16),
                pltpu.VMEM((2, slots, rows + 2 * STEP, cols // 2, ch), BF16),
                pltpu.SemaphoreType.DMA((slots, rows // 8)),
            ],
            compiler_params=params,
            cost_estimate=pl.CostEstimate(
                flops=2 * 9 * slots * rows * cols * ch * ch,
                bytes_accessed=8 << 20,
                transcendentals=0,
            ),
            name="input_grad",
        )(neighbours, shifted, masks, grad_across, grad_pair, cot_in, turned_taps)

    scale_factor = 1.0 / (rows * math.sqrt(slots * count))
    if own is None:
        summed = scatter_sum(dw, device)
        layer_output, shifted, masks, turned_taps = gradient_call(grad_edge)
        return layer_output, input_grad_call(shifted, masks, turned_taps), summed * scale_factor

    wide = 9 * ch
    recv = permute(dw, lambda i, n: i ^ 1)
    (keep,) = pl.pallas_call(
        keep_kernel,
        out_shape=(shape_f32(rank, wide),),
        in_specs=[VMEM] * 4,
        out_specs=(VMEM,),
        compiler_params=params,
        cost_estimate=pl.CostEstimate(
            flops=9 * slots * rows * (cols + 4) * ch * ch, bytes_accessed=0, transcendentals=0
        ),
        name="keep",
    )(windows, turned, edge_windows, edge_turned)
    whole = (outer, middle, own, wide)
    keep, *sends = small_call(
        functools.partial(split_kernel, 2),
        (shape_f32(outer, own, wide), *[shape_bf16(outer, own, wide)] * (middle - 1)),
        "middle_terms", keep.reshape(whole), recv.reshape(whole),
    )
    recvs = [permute(sends[k - 1], lambda i, n, k=k: i ^ (k * 2)) for k in range(1, middle)]
    keep, grad_edge = lax.optimization_barrier((keep, grad_edge))
    layer_output, shifted, masks, turned_taps = gradient_call(grad_edge)
    keep, *recvs, shifted = lax.optimization_barrier((keep, *recvs, shifted))
    keep, *sends = small_call(
        functools.partial(split_kernel, 2 * middle),
        (shape_f32(1, own, wide), *[shape_bf16(1, own, wide)] * (outer - 1)),
        "outer_terms", keep[None], *[recv[None] for recv in recvs],
    )
    keep, shifted = lax.optimization_barrier((keep, shifted))
    recvs = [
        permute(sends[k - 1], lambda i, n, k=k: i ^ (k * 2 * middle))
        for k in reversed(range(1, outer))
    ]
    input_grad = input_grad_call(shifted, masks, turned_taps)
    (summed,) = small_call(
        functools.partial(last_kernel, scale_factor),
        (shape_f32(1, own, wide),),
        "last_sum", keep, *recvs,
    )
    return layer_output, input_grad, summed[0]


def solution(mesh):
    return jax.shard_map(
        shards,
        mesh=mesh,
        in_specs=(
            P(("groups", "tiles"), None, None, None),
            P(("groups", "tiles"), None, None, None),
            P(),
            P("tiles", None),
            P("tiles", None, None),
        ),
        out_specs=(
            P(("groups", "tiles"), None, None, None),
            P(("groups", "tiles"), None, None, None),
            P(("groups", "tiles"), None),
        ),
        check_vma=False,
    )
```
